32 devices in a mesh: groups: 2 (over y), seq: 4 (over z), head: 2 (over x), prompt: 2 (over core).
Axes of the slice: x: 2, y: 2, z: 4, core: 2. Of those that a mesh axis runs over, the one named last changes fastest.
Arguments:
- prompt_queries: bfloat16 [4, 512, 2048], P(('groups', 'prompt'), 'seq', 'head'), parts along dimension 0, may hold values from -6 to 6
- prompt_keys: bfloat16 [4, 512, 2048], P(('groups', 'prompt'), 'seq', 'head'), parts along dimension 0, may hold values from -20 to 20
- prompt_values: bfloat16 [4, 512, 4096], P(('groups', 'prompt'), 'seq', 'head'), parts along dimension 0, may hold values from -6 to 6
- prompt_beta: float32 [4, 32, 512], P(('groups', 'prompt'), 'head', 'seq'), parts along dimension 0, may hold values from 0.005 to 0.15
- prompt_decay: float32 [4, 32, 512], P(('groups', 'prompt'), 'head', 'seq'), parts along dimension 0, may hold values from -0.7 to 0
- suffix_queries: bfloat16 [32, 256, 2048], P(('groups', 'seq', 'prompt'), None, 'head'), parts along dimension 0, may hold values from -6 to 6
- suffix_keys: bfloat16 [32, 256, 2048], P(('groups', 'seq', 'prompt'), None, 'head'), parts along dimension 0, may hold values from -20 to 20
- suffix_values: bfloat16 [32, 256, 4096], P(('groups', 'seq', 'prompt'), None, 'head'), parts along dimension 0, may hold values from -6 to 6
- suffix_beta: float32 [32, 32, 256], P(('groups', 'seq', 'prompt'), 'head'), parts along dimension 0, may hold values from 0.005 to 0.15
- suffix_decay: float32 [32, 32, 256], P(('groups', 'seq', 'prompt'), 'head'), parts along dimension 0, may hold values from -0.2 to 0
- norm_gain: float32 [128], replicated, may hold values from 0.25 to 1.75
- slot_branch: int32 [32], P('groups'), parts along dimension 0, may hold values from 0 to 15, each once
- branch_length: int32 [32], P('groups'), parts along dimension 0, may hold values from 1 to 256, 2048 in all
- branch_prompt: int32 [32], P('groups'), parts along dimension 0, may hold values from 0 to 1
Outputs:
- prompt_out: bfloat16 [4, 512, 4096], P(('groups', 'prompt'), 'seq', 'head'), parts along dimension 0
- suffix_out: bfloat16 [32, 256, 4096], P(('groups', 'seq', 'prompt'), None, 'head'), parts along dimension 0
The draws below stay inside these ranges and needn't reach their ends.
There are 2 independent parts, one for each index of `groups`. The reference program is written for one: setup_inputs(seed, part) draws one part's arguments, and reference() takes and returns one part's arrays. A program takes and returns all parts, laid end to end along the dimension named above; an argument that names none is the same for every part. Nothing has to cross between parts.
Inputs may be any that keep to these rules, and one draw needn't show every extreme that they name: slot_branch names every branch exactly once. `branch_length`: the lengths sum to 2048 and one of them is exactly 256.
All inputs are finite; a program needn't handle non-finite values.
Results may differ from the reference program's by a relative error of at most 0.0067.
Values sent between devices are 32-bit elements; how exact they have to be, the bound alone decides.
No kernel may reach another device: no remote copies, remote signals or barrier semaphores. Data moves between devices by JAX's collectives and lax.ppermute only.
A program may use at most 128 MiB of HBM per device.

```python
import math
import jax
import jax.numpy as jnp
import numpy as np
from jax import lax

DK = 128
DV = 128
OUTPUT_HEAD_NUM = 32
HK = 16
TOK_DEV = 128
SUF = 256
QUERY_TEXT_SPAN = 512
PROMPT_COUNT = 2
BRANCHES = 16


def fast_heads(key):
    head_picks = jax.random.randint(jax.random.fold_in(key, 101), (OUTPUT_HEAD_NUM,), 0, 2)
    return head_picks == 0


def channel_scales(key):
    return jnp.exp(jax.random.uniform(jax.random.fold_in(key, 202), (HK * DK,), jnp.float32, -1.2, 1.2))


def key_draw(key, noise_generator_key, shape):
    noise_part = jnp.clip(jax.random.normal(jax.random.fold_in(key, noise_generator_key), shape, jnp.float32), -4.0, 4.0)
    return (noise_part * channel_scales(key)).astype(jnp.bfloat16)


def beta_draw(key, noise_generator_key, prefix_number, length):
    quick_channel_selector = fast_heads(key)[None, :, None]
    quick_forget_bound = jax.random.uniform(jax.random.fold_in(key, noise_generator_key), (prefix_number, OUTPUT_HEAD_NUM, 1), jnp.float32, 0.02, 0.1)
    gentle = jnp.exp(jax.random.uniform(jax.random.fold_in(key, noise_generator_key + 1), (prefix_number, OUTPUT_HEAD_NUM, 1), jnp.float32, -4.6, -3.0))
    jitter = jax.random.uniform(jax.random.fold_in(key, noise_generator_key + 2), (prefix_number, OUTPUT_HEAD_NUM, length), jnp.float32, 0.6, 1.4)
    return jnp.where(quick_channel_selector, quick_forget_bound, gentle) * jitter


def decay_draw(key, noise_generator_key, prefix_number, length, tile_extent):
    quick_channel_selector = fast_heads(key)[None, :, None]
    tile_total = length // tile_extent
    spike_span = min(32, tile_extent // 4)
    quick_forget_bound = jax.random.uniform(jax.random.fold_in(key, noise_generator_key), (prefix_number, OUTPUT_HEAD_NUM, 1), jnp.float32, 1.0 / 50.0, 1.0 / 40.0)
    spike_start_slot = jax.random.randint(jax.random.fold_in(key, noise_generator_key + 3), (prefix_number, OUTPUT_HEAD_NUM, tile_total), 0, tile_extent - spike_span + 1)
    spike_start_slot = jnp.repeat(spike_start_slot, tile_extent, axis=2)
    tile_offset = (jnp.arange(length, dtype=jnp.int32) % tile_extent)[None, None, :]
    within_spike = (tile_offset >= spike_start_slot) & (tile_offset < spike_start_slot + spike_span)
    forget_lower_bound = jnp.where(quick_channel_selector & within_spike, quick_forget_bound, 0.25 / QUERY_TEXT_SPAN)
    spread_factor = jnp.exp(jax.random.uniform(jax.random.fold_in(key, noise_generator_key + 1), (prefix_number, OUTPUT_HEAD_NUM, tile_total), jnp.float32, -0.7, 0.7))
    spread_factor = jnp.repeat(spread_factor, tile_extent, axis=2)
    jitter = jax.random.uniform(jax.random.fold_in(key, noise_generator_key + 2), (prefix_number, OUTPUT_HEAD_NUM, length), jnp.float32, 0.7, 1.3)
    return -forget_lower_bound * spread_factor * jitter


def draw_prompt_keys(key, part):
    return key_draw(key, 211, (PROMPT_COUNT, QUERY_TEXT_SPAN, HK * DK))


def draw_suffix_keys(key, part):
    return key_draw(key, 221, (BRANCHES, SUF, HK * DK))


def draw_prompt_beta(key, part):
    return beta_draw(key, 411, PROMPT_COUNT, QUERY_TEXT_SPAN)


def draw_suffix_beta(key, part):
    return beta_draw(key, 421, BRANCHES, SUF)


def draw_prompt_decay(key, part):
    smoothed_decay = decay_draw(key, 311, PROMPT_COUNT, QUERY_TEXT_SPAN, TOK_DEV)
    spike_positions = jax.random.randint(jax.random.fold_in(key, 321), (PROMPT_COUNT, OUTPUT_HEAD_NUM, 3), 0, QUERY_TEXT_SPAN)
    place_indices = jnp.arange(QUERY_TEXT_SPAN, dtype=jnp.int32)
    spike_events = jnp.any(place_indices[None, None, :, None] == spike_positions[:, :, None, :], axis=-1)
    spike_decays = jnp.log(jax.random.uniform(jax.random.fold_in(key, 322), (PROMPT_COUNT, OUTPUT_HEAD_NUM, QUERY_TEXT_SPAN), jnp.float32, 0.5, 0.8))
    return jnp.where(spike_events, spike_decays, smoothed_decay)


def draw_suffix_decay(key, part):
    return decay_draw(key, 331, BRANCHES, SUF, SUF)


def with_ends(values, own_key, least, largest):
    index_at = [jax.random.randint(jax.random.fold_in(own_key, axis), (), 0, length) for axis, length in enumerate(values.shape)]
    main_axis = values.shape.index(max(values.shape))
    neighbour = index_at[:main_axis] + [(index_at[main_axis] + 1) % values.shape[main_axis]] + index_at[main_axis + 1:]
    return values.at[tuple(index_at)].set(least).at[tuple(neighbour)].set(largest)


def level_of(stream_key, dims, shards, smallest, top_value):
    gain, own = 1.0, jax.random.fold_in(stream_key, 6)
    for dim, shards_of in shards:
        heights = jnp.exp(jax.random.uniform(jax.random.fold_in(own, dim), (shards_of,), jnp.float32, smallest / len(shards), top_value / len(shards)))
        gain = gain * jnp.repeat(heights, dims[dim] // shards_of).reshape([-1 if axis == dim else 1 for axis in range(len(dims))])
    return gain


def length_profile(count, total, bound, slope):
    weights = [(1 << 20) // math.isqrt(grade ** slope) + 1 for grade in range(2, count + 1)]
    rest, holding = total - bound - (count - 1), [1] * (count - 1)
    while rest > 0:
        candidates = [i for i in range(count - 1) if holding[i] < bound]
        whole, left = sum([weights[i] for i in candidates]), rest
        for i in candidates:
            extra = min(bound - holding[i], max(1, left * weights[i] // whole), rest)
            holding[i] = holding[i] + extra
            rest = rest - extra
    return np.array([bound] + holding)


def ragged_sizes(key, number_of, total, most, skew):
    if number_of == 2:
        one = jax.random.randint(key, (), max(1, total - most), min(most, total - 1) + 1)
        return jnp.stack([one, total - one])
    sizes = jnp.asarray(length_profile(number_of, total, most, skew), jnp.int32)
    pairs = (number_of - 1) // 2
    source_of, receiver = sizes[1:1 + 2 * pairs:2], sizes[2:2 + 2 * pairs:2]
    margin = jnp.minimum(source_of - 1, most - receiver)
    shifted = jax.random.randint(jax.random.fold_in(key, 1), (pairs,), 0, 1 << 20) % (margin + 1)
    sizes = sizes.at[1:1 + 2 * pairs:2].set(source_of - shifted).at[2:2 + 2 * pairs:2].set(receiver + shifted)
    return sizes[jax.random.permutation(jax.random.fold_in(key, 2), number_of)]


def centred(own_key, extent, width, most, cuts=(), kind=jnp.bfloat16):
    entries = width * jax.random.normal(own_key, extent, jnp.float32)
    if cuts:
        entries = entries * level_of(own_key, extent, cuts, -0.22, 0.18)
    return jnp.clip(entries, -most, most).astype(kind)


def setup_inputs(seed: int = 0, part: int = 0) -> dict:
    streams_of = jax.random.split(jax.random.key(seed), 15)
    own_keys = jax.random.split(jax.random.fold_in(streams_of[14], part), 15)
    prompt_queries = centred(own_keys[0], (PROMPT_COUNT, QUERY_TEXT_SPAN, HK * DK), 1.0, 6.0, ((0, 2), (1, 4), (2, 2)))
    prompt_keys = draw_prompt_keys(jax.random.fold_in(jax.random.fold_in(streams_of[14], part), 71), part)
    prompt_values = centred(own_keys[2], (PROMPT_COUNT, QUERY_TEXT_SPAN, OUTPUT_HEAD_NUM * DV), 1.0, 6.0, ((0, 2), (1, 4), (2, 2)))
    prompt_beta = draw_prompt_beta(jax.random.fold_in(jax.random.fold_in(streams_of[14], part), 71), part)
    prompt_decay = draw_prompt_decay(jax.random.fold_in(jax.random.fold_in(streams_of[14], part), 71), part)
    suffix_queries = centred(own_keys[5], (BRANCHES, SUF, HK * DK), 1.0, 6.0, ((0, 8), (2, 2)))
    suffix_keys = draw_suffix_keys(jax.random.fold_in(jax.random.fold_in(streams_of[14], part), 71), part)
    suffix_values = centred(own_keys[7], (BRANCHES, SUF, OUTPUT_HEAD_NUM * DV), 1.0, 6.0, ((0, 8), (2, 2)))
    suffix_beta = draw_suffix_beta(jax.random.fold_in(jax.random.fold_in(streams_of[14], part), 71), part)
    suffix_decay = draw_suffix_decay(jax.random.fold_in(jax.random.fold_in(streams_of[14], part), 71), part)
    norm_gain = jnp.clip(1.0 + 0.15 * jax.random.normal(streams_of[10], (DV,), jnp.float32), 0.25, 1.75)
    slot_branch = jax.random.permutation(own_keys[11], BRANCHES).astype(jnp.int32)
    branch_length = ragged_sizes(own_keys[12], BRANCHES, BRANCHES * SUF // 2, SUF, 2).astype(jnp.int32)
    branch_prompt = with_ends(jax.random.randint(own_keys[13], (BRANCHES,), 0, PROMPT_COUNT), jax.random.fold_in(own_keys[13], 1), 0, PROMPT_COUNT - 1).astype(jnp.int32)
    return {"prompt_queries": prompt_queries, "prompt_keys": prompt_keys, "prompt_values": prompt_values, "prompt_beta": prompt_beta, "prompt_decay": prompt_decay, "suffix_queries": suffix_queries, "suffix_keys": suffix_keys, "suffix_values": suffix_values, "suffix_beta": suffix_beta, "suffix_decay": suffix_decay, "norm_gain": norm_gain, "slot_branch": slot_branch, "branch_length": branch_length, "branch_prompt": branch_prompt}


HIGH_PRECISION = lax.Precision.HIGHEST
EPS_NORM = 1e-06

def unit_rows(vectors):
    widened = vectors.astype(jnp.float32)
    factor = lax.rsqrt(lax.optimization_barrier(jnp.sum(widened * widened, axis=-1, keepdims=True)) + EPS_NORM)
    return (widened * factor).astype(jnp.bfloat16)

def normed(raw_out, norm_gain):
    inv_rms = lax.rsqrt(lax.optimization_barrier(jnp.mean(raw_out * raw_out, axis=-1, keepdims=True)) + EPS_NORM)
    return (raw_out * inv_rms * norm_gain).astype(jnp.bfloat16)

def prepare(queries, key_rows, value_rows, beta_rows, decay_rows):
    tokens = queries.shape[0]
    query_unit = jnp.repeat(unit_rows(queries.reshape(tokens, HK, DK)), OUTPUT_HEAD_NUM // HK, axis=1)
    key_unit = jnp.repeat(unit_rows(key_rows.reshape(tokens, HK, DK)), OUTPUT_HEAD_NUM // HK, axis=1)
    return (query_unit, key_unit, value_rows.reshape(tokens, OUTPUT_HEAD_NUM, DV), beta_rows.T, decay_rows.T)

def run_chain(start_state, query_unit, key_unit, value_rows, beta_rows, decay_rows):

    def advance(present_state, inputs):
        query_current, key_now, value_now, beta_now, decay_now = inputs
        key_single = key_now.astype(jnp.float32)
        faded_state = jnp.exp(decay_now)[:, None, None] * present_state
        retrieved_value = jnp.einsum('te,tei->ti', key_single, faded_state, precision=HIGH_PRECISION)
        written = beta_now[:, None] * (value_now.astype(jnp.float32) - retrieved_value)
        present_state = faded_state + key_single[:, :, None] * written[:, None, :]
        output_rows = jnp.einsum('te,tei->ti', query_current.astype(jnp.float32), present_state, precision=HIGH_PRECISION)
        return (present_state, output_rows)
    return lax.scan(advance, start_state, (query_unit, key_unit, value_rows, beta_rows, decay_rows))

def reference(prompt_queries, prompt_keys, prompt_values, prompt_beta, prompt_decay, suffix_queries, suffix_keys, suffix_values, suffix_beta, suffix_decay, norm_gain, slot_branch, branch_length, branch_prompt):
    zero_state = jnp.zeros((OUTPUT_HEAD_NUM, DK, DV), jnp.float32)
    finals = []
    prompt_rows = []
    for prompt_index in range(PROMPT_COUNT):
        prepared = prepare(prompt_queries[prompt_index], prompt_keys[prompt_index], prompt_values[prompt_index], prompt_beta[prompt_index], prompt_decay[prompt_index])
        final_state, output_rows = run_chain(zero_state, prepared[0], prepared[1], prepared[2], prepared[3], prepared[4])
        finals.append(final_state)
        prompt_rows.append(normed(output_rows, norm_gain).reshape(QUERY_TEXT_SPAN, OUTPUT_HEAD_NUM * DV))
    prompt_out = jnp.stack(prompt_rows)
    final_states = jnp.stack(finals)
    slot_index = slot_branch.astype(jnp.int32)
    lengths = branch_length[slot_index]
    owners = branch_prompt[slot_index].astype(jnp.int32)
    seed_states = final_states[owners]

    def run_slot(seed_state, queries, key_rows, value_rows, beta_rows, decay_rows):
        prepared = prepare(queries, key_rows, value_rows, beta_rows, decay_rows)
        ignored, output_rows = run_chain(seed_state, prepared[0], prepared[1], prepared[2], prepared[3], prepared[4])
        return normed(output_rows, norm_gain)
    suffix_rows = jax.vmap(run_slot)(seed_states, suffix_queries, suffix_keys, suffix_values, suffix_beta, suffix_decay)
    live_rows = jnp.arange(SUF, dtype=jnp.int32)[None, :] < lengths[:, None]
    suffix_out = jnp.where(live_rows[:, :, None, None], suffix_rows, jnp.zeros((), jnp.bfloat16)).reshape(BRANCHES, SUF, OUTPUT_HEAD_NUM * DV)
    return (prompt_out, suffix_out)
```

```python
import functools

import jax
import jax.numpy as jnp
from jax import lax
from jax.experimental import pallas as pl
from jax.experimental.pallas import tpu as pltpu
from jax.sharding import PartitionSpec as P

DK = 128
DV = 128
CH = 128
W2 = 2 * DV
EPS_NORM = 1e-06
HIGH = lax.Precision.HIGHEST
VMEM = 56 * 1024 * 1024


def mm(left, right):
    return lax.dot_general(left, right, (((1,), (0,)), ((), ())), preferred_element_type=jnp.float32)


def diag2(pair):
    zero = jnp.zeros((pair.shape[0], DV), pair.dtype)
    top = jnp.concatenate([pair[:, :DV], zero], axis=1)
    low = jnp.concatenate([zero, pair[:, DV:]], axis=1)
    return jnp.concatenate([top, low], axis=0)


def low16(value):
    return value.astype(jnp.bfloat16)


def lanes2(col_a, col_b):
    shape = (col_a.shape[0], DV)
    return jnp.concatenate(
        [jnp.broadcast_to(col_a, shape), jnp.broadcast_to(col_b, shape)], axis=1
    )


def unit_rows(vectors):
    wide = vectors.astype(jnp.float32)
    factor = lax.rsqrt(jnp.sum(wide * wide, axis=-1, keepdims=True) + EPS_NORM)
    return low16(wide * factor)


def apply_pair(transfer, state, offset):
    t_hi = low16(transfer)
    t_lo = low16(transfer - t_hi.astype(jnp.float32))
    s_hi = low16(state)
    s_lo = low16(state - s_hi.astype(jnp.float32))
    hi = diag2(s_hi)
    return mm(t_hi, hi) + mm(t_lo, hi) + mm(t_hi, diag2(s_lo)) + offset


def gate_tables(beta, decay):
    rows = lax.broadcasted_iota(jnp.int32, (CH, CH), 0)
    cols = lax.broadcasted_iota(jnp.int32, (CH, CH), 1)
    upper = jnp.where(rows <= cols, 1.0, 0.0).astype(jnp.float32)
    cum = lax.dot_general(
        decay, upper, (((1,), (0,)), ((), ())), precision=HIGH, preferred_element_type=jnp.float32
    )
    return beta.T, cum, cum.T


def chunk_terms(chains):
    rows = lax.broadcasted_iota(jnp.int32, (CH, W2), 0)
    cols = jnp.bitwise_and(lax.broadcasted_iota(jnp.int32, (CH, W2), 1), CH - 1)
    causal = rows >= cols
    strict = rows > cols
    eye = jnp.where(rows == cols, 1.0, 0.0).astype(jnp.float32)
    apart = jnp.bitwise_xor(rows, cols)
    near = strict & (apart < 8)

    state = []
    for q, k, v, beta_c, cum_r, cum_c in chains:
        qn = unit_rows(q)
        kn = unit_rows(k)
        kf = kn.astype(jnp.float32)
        kt = kf.T
        state.append((qn, kn, kf, kt))
    grams = [mm(jnp.concatenate([kn, qn], axis=0), low16(kt)) for qn, kn, kf, kt in state]
    lows, attns = [], []
    for (q, k, v, beta_c, cum_r, cum_c), gram in zip(chains, grams):
        kk = gram[:CH]
        qk = gram[CH:]
        row = jnp.concatenate([cum_r[0:1], cum_r[1:2]], axis=1)
        ratio = jnp.exp(jnp.where(causal, lanes2(cum_c[:, 0:1], cum_c[:, 1:2]) - row, -1e30))
        scaled = lanes2(beta_c[:, 0:1], beta_c[:, 1:2]) * ratio
        lows.append(jnp.where(strict, scaled * jnp.concatenate([kk, kk], axis=1), 0.0))
        attns.append(low16(ratio * jnp.concatenate([qk, qk], axis=1)))
    lows16 = [low16(low) for low in lows]
    nil = [jnp.where(near, -low, 0.0) for low in lows]
    nil16 = [low16(n) for n in nil]
    sq = [low16(mm(n, diag2(n))) for n in nil16]
    base = [eye + n for n in nil]
    both = [mm(jnp.concatenate([s, low16(b)], axis=0), diag2(s)) for s, b in zip(sq, base)]
    base = [b + x[CH:] for b, x in zip(base, both)]
    inv = [b + mm(low16(b), diag2(low16(x[:CH]))) for b, x in zip(base, both)]
    for level in (3, 4, 5, 6):
        here = lax.shift_right_logical(apart, level) == 1
        inv16 = [low16(i) for i in inv]
        mid = [
            low16(mm(jnp.where(here, low, jnp.zeros_like(low)), diag2(i)))
            for low, i in zip(lows16, inv16)
        ]
        inv = [i - mm(i16, diag2(m)) for i, i16, m in zip(inv, inv16, mid)]
    out = []
    stage = []
    for (q, k, v, beta_c, cum_r, cum_c), (qn, kn, kf, kt), i in zip(chains, state, inv):
        grow = jnp.exp(cum_c)
        bg = beta_c * grow
        i16 = low16(i)
        kf2 = jnp.concatenate([kf, kf], axis=1)
        w = mm(i16, diag2(low16(kf2 * lanes2(bg[:, 0:1], bg[:, 1:2]))))
        u = mm(i16, diag2(low16(v.astype(jnp.float32) * lanes2(beta_c[:, 0:1], beta_c[:, 1:2]))))
        stage.append((grow, low16(w), low16(u)))
    for (q, k, v, beta_c, cum_r, cum_c), (qn, kn, kf, kt), attn, (grow, w, u) in zip(
        chains, state, attns, stage
    ):
        last = cum_r[:, CH - 1 : CH]
        tail = jnp.exp(last - cum_r)
        tail_k = low16(
            jnp.concatenate([kt, kt], axis=1) * jnp.concatenate([tail[0:1], tail[1:2]], axis=1)
        )
        left = jnp.concatenate([attn, tail_k], axis=0)
        by_w = mm(left, diag2(w))
        by_u = mm(left, diag2(u))
        qf = qn.astype(jnp.float32)
        a = jnp.concatenate([qf, qf], axis=1) * lanes2(grow[:, 0:1], grow[:, 1:2]) - by_w[:CH]
        end = jnp.exp(last)
        shrink = jnp.concatenate(
            [jnp.broadcast_to(end[0:1], (1, DV)), jnp.broadcast_to(end[1:2], (1, DV))], axis=1
        )
        out.append((a, by_u[:CH], eye * shrink - by_w[CH:], by_u[CH:]))
    return out


def prompt_kernel(first, pairs, q_ref, k_ref, v_ref, beta_ref, decay_ref, to_ref, a_ref, b_ref):
    heads = slice(2 * first, 2 * (first + pairs))
    beta_c, cum_r, cum_c = gate_tables(beta_ref[0, heads, :], decay_ref[0, heads, :])
    chains = []
    for p in range(pairs):
        chains.append(
            (
                q_ref[0, :, p * DK : (p + 1) * DK],
                k_ref[0, :, p * DK : (p + 1) * DK],
                v_ref[0, :, p * W2 : (p + 1) * W2],
                beta_c[:, 2 * p : 2 * p + 2],
                cum_r[2 * p : 2 * p + 2],
                cum_c[:, 2 * p : 2 * p + 2],
            )
        )
    for p, (a, b, transfer, offset) in enumerate(chunk_terms(chains)):
        a_ref[:, p * W2 : (p + 1) * W2] = low16(a)
        b_ref[:, p * W2 : (p + 1) * W2] = b
        to_ref[0, p] = transfer
        to_ref[1, p] = offset


def prompt_terms(first, pairs, q, k, v, beta, decay):
    at = first // pairs
    return pl.pallas_call(
        functools.partial(prompt_kernel, first, pairs),
        grid=(1,),
        in_specs=[
            pl.BlockSpec((1, CH, pairs * DK), lambda i: (0, 0, at)),
            pl.BlockSpec((1, CH, pairs * DK), lambda i: (0, 0, at)),
            pl.BlockSpec((1, CH, pairs * W2), lambda i: (0, 0, at)),
            pl.BlockSpec(beta.shape, lambda i: (0, 0, 0)),
            pl.BlockSpec(decay.shape, lambda i: (0, 0, 0)),
        ],
        out_specs=[
            pl.BlockSpec((2, pairs, DK, W2), lambda i: (0, 0, 0, 0)),
            pl.BlockSpec((CH, pairs * W2), lambda i: (0, 0)),
            pl.BlockSpec((CH, pairs * W2), lambda i: (0, 0)),
        ],
        out_shape=[
            jax.ShapeDtypeStruct((2, pairs, DK, W2), jnp.float32),
            jax.ShapeDtypeStruct((CH, pairs * W2), jnp.bfloat16),
            jax.ShapeDtypeStruct((CH, pairs * W2), jnp.float32),
        ],
        compiler_params=pltpu.CompilerParams(vmem_limit_bytes=VMEM),
        name="prompt_terms",
    )(q, k, v, beta, decay)


def suffix_kernel(first, unit, q_ref, k_ref, v_ref, beta_ref, decay_ref, a_ref, b_ref):
    spans = q_ref.shape[1] // CH
    heads = slice(2 * first, 2 * (first + unit))
    chains = []
    for s in range(spans):
        at = slice(s * CH, (s + 1) * CH)
        beta_c, cum_r, cum_c = gate_tables(beta_ref[0, heads, at], decay_ref[0, heads, at])
        for p in range(unit):
            chains.append(
                (
                    q_ref[0, at, p * DK : (p + 1) * DK],
                    k_ref[0, at, p * DK : (p + 1) * DK],
                    v_ref[0, at, p * W2 : (p + 1) * W2],
                    beta_c[:, 2 * p : 2 * p + 2],
                    cum_r[2 * p : 2 * p + 2],
                    cum_c[:, 2 * p : 2 * p + 2],
                )
            )
    terms = chunk_terms(chains)
    for p in range(unit):
        lanes = slice(p * W2, (p + 1) * W2)
        a, b, transfer, offset = terms[p]
        a_ref[0, 0:CH, lanes] = low16(a)
        b_ref[0, 0:CH, lanes] = b
        for s in range(1, spans):
            a, b, t_next, o_next = terms[s * unit + p]
            a16 = low16(a)
            at = slice(s * CH, (s + 1) * CH)
            d_t = diag2(low16(transfer))
            d_o = diag2(low16(offset))
            a_ref[0, at, lanes] = low16(mm(a16, d_t))
            b_ref[0, at, lanes] = mm(a16, d_o) + b
            if s + 1 < spans:
                t16 = low16(t_next)
                transfer, offset = mm(t16, d_t), mm(t16, d_o) + o_next


def suffix_terms(first, pairs, unit, q, k, v, beta, decay):
    slots, tokens = q.shape[0], q.shape[1]
    calls = []
    for part in range(0, pairs, unit):
        at = (first + part) // unit
        calls.append(
            pl.pallas_call(
                functools.partial(suffix_kernel, first + part, unit),
                grid=(slots,),
                in_specs=[
                    pl.BlockSpec((1, tokens, unit * DK), lambda i, at=at: (i, 0, at)),
                    pl.BlockSpec((1, tokens, unit * DK), lambda i, at=at: (i, 0, at)),
                    pl.BlockSpec((1, tokens, unit * W2), lambda i, at=at: (i, 0, at)),
                    pl.BlockSpec((1,) + beta.shape[1:], lambda i: (i, 0, 0)),
                    pl.BlockSpec((1,) + decay.shape[1:], lambda i: (i, 0, 0)),
                ],
                out_specs=[
                    pl.BlockSpec((1, tokens, unit * W2), lambda i: (i, 0, 0)),
                    pl.BlockSpec((1, tokens, unit * W2), lambda i: (i, 0, 0)),
                ],
                out_shape=[
                    jax.ShapeDtypeStruct((slots, tokens, unit * W2), jnp.bfloat16),
                    jax.ShapeDtypeStruct((slots, tokens, unit * W2), jnp.float32),
                ],
                compiler_params=pltpu.CompilerParams(vmem_limit_bytes=VMEM),
                name="suffix_terms",
            )(q, k, v, beta, decay)
        )
    return calls


def step_kernel(pairs, to_ref, s_ref, out_ref):
    for p in range(pairs):
        out_ref[p] = apply_pair(to_ref[0, p], s_ref[p], to_ref[1, p])


def step(to, state):
    pairs = state.shape[0]
    return pl.pallas_call(
        functools.partial(step_kernel, pairs),
        out_shape=jax.ShapeDtypeStruct(state.shape, jnp.float32),
        compiler_params=pltpu.CompilerParams(vmem_limit_bytes=VMEM),
        name="state_step",
    )(to, state)


def step2_kernel(pairs, to_ref, far_ref, s_ref, out_ref, final_ref):
    for p in range(pairs):
        state = apply_pair(to_ref[0, p], s_ref[p], to_ref[1, p])
        out_ref[p] = state
        final_ref[p] = apply_pair(far_ref[0, p], state, far_ref[1, p])


def step2(to, far, state):
    pairs = state.shape[0]
    shape = jax.ShapeDtypeStruct(state.shape, jnp.float32)
    return pl.pallas_call(
        functools.partial(step2_kernel, pairs),
        out_shape=[shape, shape],
        compiler_params=pltpu.CompilerParams(vmem_limit_bytes=VMEM),
        name="state_step_twice",
    )(to, far, state)


def finish(a, state, b, gain2):
    raw = mm(a, diag2(low16(state))) + b
    sq = raw * raw
    parts = []
    for h in range(2):
        lanes = slice(h * DV, (h + 1) * DV)
        inv = lax.rsqrt(jnp.mean(sq[:, lanes], axis=-1, keepdims=True) + EPS_NORM)
        parts.append(raw[:, lanes] * inv)
    return jnp.concatenate(parts, axis=1) * gain2


def suffix_out_kernel(unit, slots, n_prompt, *refs):
    sb_ref, bl_ref, bp_ref, own_ref, other_ref, a_ref, b_ref, gain_ref = refs[:8]
    out_ref = refs[-1]
    me = lax.axis_index("prompt")
    rank = lax.axis_index("seq") * n_prompt + me
    branch = sb_ref[rank * slots + pl.program_id(0)]
    length = bl_ref[branch]
    mine = bp_ref[branch] == me
    gain = gain_ref[...]
    gain2 = jnp.concatenate([gain, gain], axis=1)
    tokens = a_ref.shape[1]
    live = lax.broadcasted_iota(jnp.int32, (tokens, W2), 0) < length
    for p in range(unit):
        lanes = slice(p * W2, (p + 1) * W2)
        state = jnp.where(mine, own_ref[p], other_ref[p])
        out = finish(a_ref[0, :, lanes], state, b_ref[0, :, lanes], gain2)
        out_ref[0, :, lanes] = low16(jnp.where(live, out, 0.0))


def suffix_outputs(first, index, tables, own, other, a, b, gain, so_far, width):
    slots, tokens, lanes = a.shape
    unit = lanes // W2
    at = first // unit
    smem = pl.BlockSpec(memory_space=pltpu.SMEM)
    in_specs = [
        smem,
        smem,
        smem,
        pl.BlockSpec((unit, DK, W2), lambda i: (index, 0, 0)),
        pl.BlockSpec((unit, DK, W2), lambda i: (index, 0, 0)),
        pl.BlockSpec((1, tokens, lanes), lambda i: (i, 0, 0)),
        pl.BlockSpec((1, tokens, lanes), lambda i: (i, 0, 0)),
        pl.BlockSpec((1, DV), lambda i: (0, 0)),
    ]
    args = list(tables) + [own, other, a, b, gain]
    aliases = {}
    if so_far is not None:
        in_specs.append(pl.BlockSpec(memory_space=pl.ANY))
        args.append(so_far)
        aliases = {8: 0}
    return pl.pallas_call(
        functools.partial(suffix_out_kernel, unit, slots, lax.axis_size("prompt")),
        grid=(slots,),
        in_specs=in_specs,
        out_specs=pl.BlockSpec((1, tokens, lanes), lambda i: (i, 0, at)),
        out_shape=jax.ShapeDtypeStruct((slots, tokens, width), jnp.bfloat16),
        input_output_aliases=aliases,
        compiler_params=pltpu.CompilerParams(vmem_limit_bytes=VMEM),
        name="suffix_out",
    )(*args)


def prompt_out_kernel(pairs, s_ref, a_ref, b_ref, gain_ref, *refs):
    out_ref = refs[-1]
    gain = gain_ref[...]
    gain2 = jnp.concatenate([gain, gain], axis=1)
    for p in range(pairs):
        lanes = slice(p * W2, (p + 1) * W2)
        out_ref[0, :, lanes] = low16(finish(a_ref[:, lanes], s_ref[p], b_ref[:, lanes], gain2))


def prompt_outputs(first, state, a, b, gain, so_far, width):
    pairs = state.shape[0]
    at = first // pairs
    in_specs = [
        pl.BlockSpec(state.shape, lambda i: (0, 0, 0)),
        pl.BlockSpec(a.shape, lambda i: (0, 0)),
        pl.BlockSpec(b.shape, lambda i: (0, 0)),
        pl.BlockSpec((1, DV), lambda i: (0, 0)),
    ]
    args = [state, a, b, gain]
    aliases = {}
    if so_far is not None:
        in_specs.append(pl.BlockSpec(memory_space=pl.ANY))
        args.append(so_far)
        aliases = {4: 0}
    return pl.pallas_call(
        functools.partial(prompt_out_kernel, pairs),
        grid=(1,),
        in_specs=in_specs,
        out_specs=pl.BlockSpec((1, CH, pairs * W2), lambda i: (0, 0, at)),
        out_shape=jax.ShapeDtypeStruct((1, CH, width), jnp.bfloat16),
        input_output_aliases=aliases,
        compiler_params=pltpu.CompilerParams(vmem_limit_bytes=VMEM),
        name="prompt_out",
    )(*args)


def pair_product(left, right):
    pairs = left.shape[0]
    left = left.reshape(pairs, DK, 2, DK)
    right = right.reshape(pairs, DK, 2, DV)
    return jnp.einsum("pihj,pjhv->pihv", left, right, precision=HIGH).reshape(pairs, DK, W2)


def exchange(to):
    count = lax.axis_size("seq")
    half = count // 2
    here = lax.axis_index("seq")
    sending = to
    far = None
    for j in range(half - 1):
        arrived = lax.ppermute(sending, "seq", [(j, j + 1), (count - 1 - j, count - 2 - j)])
        far = arrived if far is None else far + arrived
        prefix = step(to, arrived[1])
        if j + 2 < half:
            joined = jnp.stack(
                [pair_product(arrived[0], to[0]), pair_product(arrived[0], to[1]) + arrived[1]]
            )
            sending = jnp.where(here < half, jnp.stack([prefix, prefix]), joined)
    middle = lax.ppermute(prefix, "seq", [(half - 1, half)])
    state_out, final_mid = step2(to, far, middle)
    back = lax.ppermute(final_mid, "seq", [(half, half - 1)])
    incoming = jnp.where(here == half, middle, jnp.where(here < half, far[1], 0.0))
    final = jnp.where(here == half, final_mid, back)
    left_out = back
    for j in range(half - 1):
        arrived = lax.ppermute(
            jnp.where(here < half, left_out, state_out),
            "seq",
            [(half - 1 - j, half - 2 - j), (half + j, half + j + 1)],
        )
        state_out = step(to, arrived)
        left_out = arrived
        right = here == half + j + 1
        if j + 2 < half:
            right_final = pair_product(far[0], state_out) + far[1]
        else:
            right_final = state_out
        incoming = jnp.where(right, arrived, incoming)
        final = jnp.where(right, right_final, jnp.where(here == half - 2 - j, arrived, final))
    return incoming, final


def split_pairs(pairs):
    half = max(1, pairs // 2)
    return (half,) * (pairs // half)


def local(
    prompt_queries,
    prompt_keys,
    prompt_values,
    prompt_beta,
    prompt_decay,
    suffix_queries,
    suffix_keys,
    suffix_values,
    suffix_beta,
    suffix_decay,
    norm_gain,
    slot_branch,
    branch_length,
    branch_prompt,
):
    gain = norm_gain.reshape(1, DV)
    tables = (slot_branch, branch_length, branch_prompt)
    prompts = lax.axis_size("prompt")
    groups = split_pairs(prompt_values.shape[2] // W2)
    terms = []
    first = 0
    for pairs in groups:
        terms.append(
            prompt_terms(
                first, pairs, prompt_queries, prompt_keys, prompt_values, prompt_beta, prompt_decay
            )
        )
        first += pairs
    states = [exchange(to) for to, a, b in terms]
    prompt_out, suffix_out = None, None
    first = 0
    for pairs, (to, a, b), (incoming, final) in zip(groups, terms, states):
        other = lax.ppermute(final, "prompt", [(i, (i + 1) % prompts) for i in range(prompts)])
        unit = min(2, pairs)
        calls = suffix_terms(
            first,
            pairs,
            unit,
            suffix_queries,
            suffix_keys,
            suffix_values,
            suffix_beta,
            suffix_decay,
        )
        prompt_out = prompt_outputs(
            first, incoming, a, b, gain, prompt_out, prompt_values.shape[2]
        )
        for index, (a, b) in enumerate(calls):
            suffix_out = suffix_outputs(
                first + index * unit,
                index,
                tables,
                final,
                other,
                a,
                b,
                gain,
                suffix_out,
                suffix_values.shape[2],
            )
        first += pairs
    return (prompt_out, suffix_out)


def solution(mesh):
    return jax.shard_map(
        local,
        mesh=mesh,
        in_specs=(
            P(("groups", "prompt"), "seq", "head"),
            P(("groups", "prompt"), "seq", "head"),
            P(("groups", "prompt"), "seq", "head"),
            P(("groups", "prompt"), "head", "seq"),
            P(("groups", "prompt"), "head", "seq"),
            P(("groups", "seq", "prompt"), None, "head"),
            P(("groups", "seq", "prompt"), None, "head"),
            P(("groups", "seq", "prompt"), None, "head"),
            P(("groups", "seq", "prompt"), "head", None),
            P(("groups", "seq", "prompt"), "head", None),
            P(),
            P("groups"),
            P("groups"),
            P("groups"),
        ),
        out_specs=(
            P(("groups", "prompt"), "seq", "head"),
            P(("groups", "seq", "prompt"), None, "head"),
        ),
        check_vma=False,
    )
```

```python
import functools
import math

import jax
import jax.numpy as jnp
from jax import lax
from jax.experimental import pallas as pl
from jax.experimental.pallas import tpu as pltpu
from jax.sharding import PartitionSpec as P

DK = 128
DV = 128
CH = 128
W2 = 2 * DV
EPS_NORM = 1e-06
HIGH = lax.Precision.HIGHEST
VMEM = 56 * 1024 * 1024


def mm(left, right):
    return lax.dot_general(left, right, (((1,), (0,)), ((), ())), preferred_element_type=jnp.float32)


def diag2(pair):
    zero = jnp.zeros((pair.shape[0], DV), pair.dtype)
    top = jnp.concatenate([pair[:, :DV], zero], axis=1)
    low = jnp.concatenate([zero, pair[:, DV:]], axis=1)
    return jnp.concatenate([top, low], axis=0)


def low16(value):
    return value.astype(jnp.bfloat16)


def halves(value):
    high = low16(value)
    return high, low16(value - high.astype(jnp.float32))


def lanes2(col_a, col_b):
    shape = (col_a.shape[0], DV)
    return jnp.concatenate(
        [jnp.broadcast_to(col_a, shape), jnp.broadcast_to(col_b, shape)], axis=1
    )


def unit_rows(vectors):
    wide = vectors.astype(jnp.float32)
    factor = lax.rsqrt(jnp.sum(wide * wide, axis=-1, keepdims=True) + EPS_NORM)
    return low16(wide * factor)


def apply_pair(transfer, state, offset):
    t_hi, t_lo = halves(transfer)
    s_hi, s_lo = halves(state)
    hi = diag2(s_hi)
    return mm(t_hi, hi) + mm(t_lo, hi) + mm(t_hi, diag2(s_lo)) + offset


def gate_tables(decay):
    rows = lax.broadcasted_iota(jnp.int32, (CH, CH), 0)
    cols = lax.broadcasted_iota(jnp.int32, (CH, CH), 1)
    upper = jnp.where(rows <= cols, 1.0, 0.0).astype(jnp.float32)
    cum = lax.dot_general(
        decay, upper, (((1,), (0,)), ((), ())), precision=HIGH, preferred_element_type=jnp.float32
    )
    return cum, cum.T


def chunk_terms(chains):
    rows = lax.broadcasted_iota(jnp.int32, (CH, W2), 0)
    cols = jnp.bitwise_and(lax.broadcasted_iota(jnp.int32, (CH, W2), 1), CH - 1)
    causal = rows >= cols
    eye = jnp.where(rows == cols, 1.0, 0.0).astype(jnp.float32)
    eye16 = low16(eye)
    apart = jnp.bitwise_xor(rows, cols)
    strict = rows > cols
    masks = [
        low16(jnp.where(strict & (apart >= low) & (apart < high), -1.0, 0.0))
        for low, high in ((1, 8), (8, 32), (32, CH))
    ]

    heads = []
    for q, k, v, beta, cum_r, cum_c in chains:
        qn = unit_rows(q)
        kn = unit_rows(k)
        heads.append((qn, kn, low16(kn.astype(jnp.float32).T)))
    grams = [mm(jnp.concatenate([kn, qn], axis=0), kt) for qn, kn, kt in heads]
    lows, lefts, grows = [], [], []
    for (q, k, v, beta, cum_r, cum_c), (qn, kn, kt), gram in zip(chains, heads, grams):
        kk = gram[:CH]
        qk = gram[CH:]
        bcast = lanes2(cum_c[:, 0:1], cum_c[:, 1:2])
        row = jnp.concatenate([cum_r[0:1], cum_r[1:2]], axis=1)
        gate = jnp.concatenate([beta[0:1], beta[1:2]], axis=1)
        scaled = jnp.exp(jnp.where(causal, bcast - row, -1e30)) * gate
        lows.append(low16(scaled * jnp.concatenate([kk, kk], axis=1)))
        attn = scaled * jnp.concatenate([qk, qk], axis=1)
        last = jnp.concatenate([cum_r[0:1, CH - 1 :], cum_r[1:2, CH - 1 :]], axis=0)
        last = jnp.concatenate(
            [jnp.broadcast_to(last[0:1], (1, DV)), jnp.broadcast_to(last[1:2], (1, DV))], axis=1
        )
        tail = jnp.exp(last - row) * gate
        ktf = kt.astype(jnp.float32)
        lefts.append(halves(jnp.concatenate([attn, jnp.concatenate([ktf, ktf], axis=1) * tail], axis=0)))
        grows.append((jnp.exp(bcast), jnp.exp(row), jnp.exp(last)))
    nil = [low * masks[0] for low in lows]
    sq = [low16(mm(n, diag2(n))) for n in nil]
    fourth = [low16(mm(s, diag2(s))) for s in sq]
    inv = [low16(mm(eye16 + n, diag2(eye16 + s))) for n, s in zip(nil, sq)]
    inv = [low16(mm(i, diag2(eye16 + f))) for i, f in zip(inv, fourth)]
    for mask in masks[1:]:
        x = [low16(mm(i, diag2(low * mask))) for i, low in zip(inv, lows)]
        y = [low16(mm(eye16 + t, diag2(i))) for t, i in zip(x, inv)]
        z = [low16(mm(t, diag2(t))) for t in x]
        full = [mm(eye16 + t, diag2(i)) for t, i in zip(z, y)]
        inv = [low16(f) for f in full]
    ws = [
        low16(mm(low16(f * grow[1]), diag2(jnp.concatenate([kn, kn], axis=1))))
        for f, grow, (qn, kn, kt) in zip(full, grows, heads)
    ]
    us = [halves(mm(i, diag2(chain[2]))) for i, chain in zip(inv, chains)]
    by_w = [mm(left, diag2(w)) for (left, rest), w in zip(lefts, ws)]
    by_u = []
    for (left, rest), (u_hi, u_lo) in zip(lefts, us):
        hi = diag2(u_hi)
        by_u.append(mm(left, hi) + mm(rest, hi) + mm(left, diag2(u_lo)))
    out = []
    for (qn, kn, kt), grow, bw, bu in zip(heads, grows, by_w, by_u):
        qf = qn.astype(jnp.float32)
        a = jnp.concatenate([qf, qf], axis=1) * grow[0] - bw[:CH]
        out.append((a, bu[:CH], eye * grow[2] - bw[CH:], bu[CH:]))
    return out


def read_chains(pairs, heads, at, q_ref, k_ref, v_ref, beta_ref, decay_ref, slot):
    beta = beta_ref[slot, heads, at]
    cum_r, cum_c = gate_tables(decay_ref[slot, heads, at])
    return [
        (
            q_ref[slot, at, p * DK : (p + 1) * DK],
            k_ref[slot, at, p * DK : (p + 1) * DK],
            v_ref[slot, at, p * W2 : (p + 1) * W2],
            beta[2 * p : 2 * p + 2],
            cum_r[2 * p : 2 * p + 2],
            cum_c[:, 2 * p : 2 * p + 2],
        )
        for p in range(pairs)
    ]


def window(first, pairs):
    return math.gcd(first, pairs) if first else pairs


def lane_specs(arrays, first, pairs, width):
    wide = window(first, pairs)
    specs, args = [], []
    for part in range(first, first + pairs, wide):
        specs.append(
            pl.BlockSpec(arrays.shape[:2] + (wide * width,), lambda i, at=part // wide: (0, 0, at))
        )
        args.append(arrays)
    return specs, args, wide


ANY = pl.BlockSpec(memory_space=pl.ANY)


class Spans:
    def __init__(self, refs, wide, width):
        self.refs, self.size, self.width = refs, wide * width, width

    def __getitem__(self, key):
        lanes = key[-1]
        part, at = divmod(lanes.start, self.size)
        return self.refs[part][key[:-1] + (slice(at, at + lanes.stop - lanes.start),)]


def prompt_kernel(first, sizes, wide, count, *refs):
    pairs = sum(sizes)
    q_ref = Spans(refs[:count], wide, DK)
    k_ref = Spans(refs[count : 2 * count], wide, DK)
    v_ref = Spans(refs[2 * count : 3 * count], wide, W2)
    beta_ref, decay_ref = refs[3 * count : 3 * count + 2]
    outs = refs[len(refs) - 2 - len(sizes) :]
    heads = slice(2 * first, 2 * (first + pairs))
    chains = read_chains(
        pairs, heads, slice(0, CH), q_ref, k_ref, v_ref, beta_ref, decay_ref, 0
    )
    places = [(c, p) for c, size in enumerate(sizes) for p in range(size)]
    for p, (a, b, transfer, offset) in enumerate(chunk_terms(chains)):
        outs[-2][:, p * W2 : (p + 1) * W2] = low16(a)
        outs[-1][:, p * W2 : (p + 1) * W2] = low16(b)
        chunk, at = places[p]
        outs[chunk][0, at] = transfer
        outs[chunk][1, at] = offset


def prompt_terms(first, sizes, q, k, v, beta, decay, after=()):
    pairs = sum(sizes)
    q_specs, q_args, wide = lane_specs(q, first, pairs, DK)
    k_specs, k_args, wide = lane_specs(k, first, pairs, DK)
    v_specs, v_args, wide = lane_specs(v, first, pairs, W2)
    *tos, a, b = pl.pallas_call(
        functools.partial(prompt_kernel, first, sizes, wide, len(q_args)),
        grid=(1,),
        in_specs=q_specs
        + k_specs
        + v_specs
        + [
            pl.BlockSpec(beta.shape, lambda i: (0, 0, 0)),
            pl.BlockSpec(decay.shape, lambda i: (0, 0, 0)),
        ]
        + [ANY] * len(after),
        out_specs=[pl.BlockSpec((2, size, DK, W2), lambda i: (0, 0, 0, 0)) for size in sizes]
        + [pl.BlockSpec((CH, pairs * W2), lambda i: (0, 0))] * 2,
        out_shape=[jax.ShapeDtypeStruct((2, size, DK, W2), jnp.float32) for size in sizes]
        + [jax.ShapeDtypeStruct((CH, pairs * W2), jnp.bfloat16)] * 2,
        compiler_params=pltpu.CompilerParams(vmem_limit_bytes=VMEM),
        name="prompt_terms",
    )(*q_args, *k_args, *v_args, beta, decay, *after)
    return tos, a, b


def suffix_kernel(first, unit, q_ref, k_ref, v_ref, beta_ref, decay_ref, *refs):
    a_ref, b_ref = refs[-2:]
    slots, tokens = q_ref.shape[:2]
    spans = tokens // CH
    heads = slice(2 * first, 2 * (first + unit))
    chains = []
    for slot in range(slots):
        for s in range(spans):
            chains += read_chains(
                unit,
                heads,
                slice(s * CH, (s + 1) * CH),
                q_ref,
                k_ref,
                v_ref,
                beta_ref,
                decay_ref,
                slot,
            )
    terms = chunk_terms(chains)
    for slot in range(slots):
        for p in range(unit):
            lanes = slice(p * W2, (p + 1) * W2)
            a, b, transfer, offset = terms[slot * spans * unit + p]
            a_ref[slot, 0:CH, lanes] = low16(a)
            b_ref[slot, 0:CH, lanes] = low16(b)
            for s in range(1, spans):
                a, b, t_next, o_next = terms[(slot * spans + s) * unit + p]
                a16 = low16(a)
                at = slice(s * CH, (s + 1) * CH)
                d_t = diag2(low16(transfer))
                d_o = diag2(low16(offset))
                a_ref[slot, at, lanes] = low16(mm(a16, d_t))
                b_ref[slot, at, lanes] = low16(mm(a16, d_o) + b)
                if s + 1 < spans:
                    t16 = low16(t_next)
                    transfer, offset = mm(t16, d_t), mm(t16, d_o) + o_next


def suffix_terms(first, unit, q, k, v, beta, decay, after=()):
    slots, tokens = q.shape[0], q.shape[1]
    at = first // unit
    return pl.pallas_call(
        functools.partial(suffix_kernel, first, unit),
        grid=(1,),
        in_specs=[
            pl.BlockSpec((slots, tokens, unit * DK), lambda i: (0, 0, at)),
            pl.BlockSpec((slots, tokens, unit * DK), lambda i: (0, 0, at)),
            pl.BlockSpec((slots, tokens, unit * W2), lambda i: (0, 0, at)),
            pl.BlockSpec(beta.shape, lambda i: (0, 0, 0)),
            pl.BlockSpec(decay.shape, lambda i: (0, 0, 0)),
        ]
        + [ANY] * len(after),
        out_specs=[pl.BlockSpec((slots, tokens, unit * W2), lambda i: (0, 0, 0))] * 2,
        out_shape=[jax.ShapeDtypeStruct((slots, tokens, unit * W2), jnp.bfloat16)] * 2,
        compiler_params=pltpu.CompilerParams(vmem_limit_bytes=VMEM),
        name="suffix_terms",
    )(q, k, v, beta, decay, *after)


def step_kernel(kinds, half, *refs):
    here = lax.axis_index("seq")
    refs = list(refs)
    counts = {"step": 2, "twice": 3}
    inputs = []
    for kind in kinds:
        inputs.append([refs.pop(0) for _ in range(counts[kind])])
    outs = refs[len(refs) - sum(2 if kind == "twice" else 1 for kind in kinds) :]
    for kind, ins in zip(kinds, inputs):
        if kind == "step":
            out = outs.pop(0)

            @pl.when(here < half)
            def _(ins=ins, out=out):
                for p in range(out.shape[0]):
                    out[p] = apply_pair(ins[0][0, p], ins[1][1, p], ins[0][1, p])

        else:
            out, final = outs.pop(0), outs.pop(0)

            @pl.when(here == half)
            def _(ins=ins, out=out, final=final):
                for p in range(out.shape[0]):
                    state = apply_pair(ins[0][0, p], ins[2][p], ins[0][1, p])
                    out[p] = state
                    final[p] = apply_pair(ins[1][0, p], state, ins[1][1, p])


def run_steps(jobs, half, after=()):
    kinds = tuple(job[0] for job in jobs)
    args, shapes = [], []
    for kind, *ins in jobs:
        args += ins
        shape = jax.ShapeDtypeStruct(ins[0].shape[1:], jnp.float32)
        shapes += [shape] * (2 if kind == "twice" else 1)
    whole = pl.BlockSpec(memory_space=pltpu.VMEM)
    outs = pl.pallas_call(
        functools.partial(step_kernel, kinds, half),
        in_specs=[whole] * len(args) + [ANY] * len(after),
        out_specs=[whole] * len(shapes),
        out_shape=shapes,
        compiler_params=pltpu.CompilerParams(vmem_limit_bytes=VMEM),
        name="state_steps",
    )(*args, *after)
    outs = list(outs)
    results = []
    for kind in kinds:
        if kind == "twice":
            results.append((outs.pop(0), outs.pop(0)))
        else:
            results.append(outs.pop(0))
    return results


def settle_kernel(half, to_ref, right_ref, mid_ref, *refs):
    here = lax.axis_index("seq")
    out_ref = refs[-1]
    lefts = refs[:half]
    for d in range(half):

        @pl.when(here == d)
        def _(d=d):
            out_ref[...] = lefts[d][...]

    @pl.when(here == half)
    def _():
        out_ref[...] = mid_ref[...]

    @pl.when(here > half)
    def _():
        for p in range(out_ref.shape[0]):
            out_ref[p] = apply_pair(to_ref[0, p], right_ref[p], to_ref[1, p])


def settle(to, right, mid, lefts, after=()):
    half = len(lefts)
    whole = pl.BlockSpec(memory_space=pltpu.VMEM)
    return pl.pallas_call(
        functools.partial(settle_kernel, half),
        in_specs=[whole] * (3 + half) + [ANY] * len(after),
        out_specs=whole,
        out_shape=jax.ShapeDtypeStruct(mid.shape, jnp.float32),
        compiler_params=pltpu.CompilerParams(vmem_limit_bytes=VMEM),
        name="settle",
    )(to, right, mid, *lefts, *after)


def finish(a, state, b, gain2):
    raw = mm(a, diag2(low16(state))) + b.astype(jnp.float32)
    sq = raw * raw
    parts = []
    for h in range(2):
        lanes = slice(h * DV, (h + 1) * DV)
        inv = lax.rsqrt(jnp.mean(sq[:, lanes], axis=-1, keepdims=True) + EPS_NORM)
        parts.append(raw[:, lanes] * inv)
    return jnp.concatenate(parts, axis=1) * gain2


def suffix_out_kernel(unit, slots, n_prompt, *refs):
    sb_ref, bl_ref, bp_ref, own_ref, other_ref, a_ref, b_ref, gain_ref = refs[:8]
    out_ref = refs[-1]
    me = lax.axis_index("prompt")
    rank = lax.axis_index("seq") * n_prompt + me
    branch = sb_ref[rank * slots + pl.program_id(0)]
    length = bl_ref[branch]
    mine = bp_ref[branch] == me
    gain = gain_ref[...]
    gain2 = jnp.concatenate([gain, gain], axis=1)
    tokens = a_ref.shape[1]
    live = lax.broadcasted_iota(jnp.int32, (tokens, W2), 0) < length
    for p in range(unit):
        lanes = slice(p * W2, (p + 1) * W2)
        state = jnp.where(mine, own_ref[p], other_ref[p])
        out = finish(a_ref[0, :, lanes], state, b_ref[0, :, lanes], gain2)
        out_ref[0, :, lanes] = low16(jnp.where(live, out, 0.0))


def suffix_outputs(first, tables, own, other, a, b, gain, so_far, width, after=()):
    slots, tokens, lanes = a.shape
    unit = lanes // W2
    at = first // unit
    smem = pl.BlockSpec(memory_space=pltpu.SMEM)
    in_specs = [
        smem,
        smem,
        smem,
        pl.BlockSpec((unit, DK, W2), lambda i: (0, 0, 0)),
        pl.BlockSpec((unit, DK, W2), lambda i: (0, 0, 0)),
        pl.BlockSpec((1, tokens, lanes), lambda i: (i, 0, 0)),
        pl.BlockSpec((1, tokens, lanes), lambda i: (i, 0, 0)),
        pl.BlockSpec((1, DV), lambda i: (0, 0)),
    ]
    args = list(tables) + [own, other, a, b, gain]
    aliases = {}
    if so_far is not None:
        in_specs.append(ANY)
        args.append(so_far)
        aliases = {8: 0}
    return pl.pallas_call(
        functools.partial(suffix_out_kernel, unit, slots, lax.axis_size("prompt")),
        grid=(slots,),
        in_specs=in_specs + [ANY] * len(after),
        out_specs=pl.BlockSpec((1, tokens, lanes), lambda i: (i, 0, at)),
        out_shape=jax.ShapeDtypeStruct((slots, tokens, width), jnp.bfloat16),
        input_output_aliases=aliases,
        compiler_params=pltpu.CompilerParams(vmem_limit_bytes=VMEM),
        name="suffix_out",
    )(*args, *after)


def prompt_out_kernel(half, skip, far_ref, mid_ref, right_ref, a_ref, b_ref, gain_ref, *refs):
    here = lax.axis_index("seq")
    out_ref = refs[-1]
    gain = gain_ref[...]
    gain2 = jnp.concatenate([gain, gain], axis=1)

    def write(state_of):
        for p in range(mid_ref.shape[0]):
            lanes = slice(p * W2, (p + 1) * W2)
            near = slice((skip + p) * W2, (skip + p + 1) * W2)
            out_ref[0, :, lanes] = low16(finish(a_ref[:, near], state_of(p), b_ref[:, near], gain2))

    @pl.when(here < half)
    def _():
        write(lambda p: far_ref[1, p])

    @pl.when(here == half)
    def _():
        write(lambda p: mid_ref[p])

    @pl.when(here > half)
    def _():
        write(lambda p: right_ref[p])


def prompt_outputs(first, skip, half, far, mid, right, a, b, gain, so_far, width, after=()):
    pairs = mid.shape[0]
    at = first // pairs
    zero3 = lambda i: (0, 0, 0)
    in_specs = [
        pl.BlockSpec(far.shape, lambda i: (0, 0, 0, 0)),
        pl.BlockSpec(mid.shape, zero3),
        pl.BlockSpec(right.shape, zero3),
        pl.BlockSpec(a.shape, lambda i: (0, 0)),
        pl.BlockSpec(b.shape, lambda i: (0, 0)),
        pl.BlockSpec((1, DV), lambda i: (0, 0)),
    ]
    args = [far, mid, right, a, b, gain]
    aliases = {}
    if so_far is not None:
        in_specs.append(ANY)
        args.append(so_far)
        aliases = {6: 0}
    return pl.pallas_call(
        functools.partial(prompt_out_kernel, half, skip),
        grid=(1,),
        in_specs=in_specs + [ANY] * len(after),
        out_specs=pl.BlockSpec((1, CH, pairs * W2), lambda i: (0, 0, at)),
        out_shape=jax.ShapeDtypeStruct((1, CH, width), jnp.bfloat16),
        input_output_aliases=aliases,
        compiler_params=pltpu.CompilerParams(vmem_limit_bytes=VMEM),
        name="prompt_out",
    )(*args, *after)


def pair_product(left, right):
    pairs = left.shape[0]
    left = left.reshape(pairs, DK, 2, DK)
    right = right.reshape(pairs, DK, 2, DV)
    return jnp.einsum("pihj,pjhv->pihv", left, right, precision=HIGH).reshape(pairs, DK, W2)


class Relay:
    def __init__(self, to):
        self.to = to
        self.count = lax.axis_size("seq")
        self.half = self.count // 2
        self.here = lax.axis_index("seq")

    def open(self):
        count, half = self.count, self.half
        sending, far = self.to, None
        for j in range(half - 1):
            arrived = lax.ppermute(sending, "seq", [(j, j + 1), (count - 1 - j, count - 2 - j)])
            far = arrived if far is None else far + arrived
            if j + 2 < half:
                prefix = pair_product(self.to[0], arrived[1]) + self.to[1]
                joined = jnp.stack(
                    [
                        pair_product(arrived[0], self.to[0]),
                        pair_product(arrived[0], self.to[1]) + arrived[1],
                    ]
                )
                sending = jnp.where(self.here < half, jnp.stack([prefix, prefix]), joined)
        self.far = far

    def prefix_job(self):
        return ("step", self.to, self.far)

    def cross(self, prefix):
        self.mid = lax.ppermute(prefix, "seq", [(self.half - 1, self.half)])

    def final_job(self):
        return ("twice", self.to, self.far, self.mid)

    def spread(self, result):
        state, self.final_mid = result
        half, count = self.half, self.count
        self.lefts = [lax.ppermute(self.final_mid, "seq", [(half, d)]) for d in range(half)]
        right = None
        for j in range(half - 1):
            arrived = lax.ppermute(state, "seq", [(half + j, half + j + 1)])
            right = arrived if right is None else right + arrived
            if j + 2 < half:
                state = pair_product(self.to[0], arrived) + self.to[1]
        self.right = right

    def settle(self, after=()):
        self.final = settle(self.to, self.right, self.final_mid, self.lefts, after)
        if self.half > 2:
            inner = (self.here > self.half) & (self.here < self.count - 1)
            done = pair_product(self.far[0], self.final) + self.far[1]
            self.final = jnp.where(inner, done, self.final)
        prompts = lax.axis_size("prompt")
        self.other = lax.ppermute(
            self.final, "prompt", [(i, (i + 1) % prompts) for i in range(prompts)]
        )


def plan_of(pairs):
    if pairs % 4:
        return [[1]] * pairs
    unit = pairs // 4
    return [[unit], [unit, unit, unit]]


def local(
    prompt_queries,
    prompt_keys,
    prompt_values,
    prompt_beta,
    prompt_decay,
    suffix_queries,
    suffix_keys,
    suffix_values,
    suffix_beta,
    suffix_decay,
    norm_gain,
    slot_branch,
    branch_length,
    branch_prompt,
):
    gain = norm_gain.reshape(1, DV)
    tables = (slot_branch, branch_length, branch_prompt)
    width = prompt_values.shape[2]
    prompt_in = (prompt_queries, prompt_keys, prompt_values, prompt_beta, prompt_decay)
    suffix_in = (suffix_queries, suffix_keys, suffix_values, suffix_beta, suffix_decay)
    half = lax.axis_size("seq") // 2

    runs = []
    first = 0
    last = ()
    for sizes in plan_of(width // W2):
        tos, a, b = prompt_terms(first, sizes, *prompt_in, after=last)
        last = (a,)
        skip = 0
        for to, size in zip(tos, sizes):
            relay = Relay(to)
            relay.open()
            runs.append((first + skip, skip, size, a, b, relay))
            skip += size
        first += skip
    total = len(runs)
    made = {}

    def make(index, after):
        if index < total:
            made[index] = suffix_terms(runs[index][0], runs[index][2], *suffix_in, after=after)
            return (made[index][0],)
        return after

    prompt_out, suffix_out = None, None

    def write_prompt(index, after):
        nonlocal prompt_out
        start, skip, size, a, b, relay = runs[index]
        prompt_out = prompt_outputs(
            start, skip, half, relay.far, relay.mid, relay.right, a, b, gain, prompt_out, width, after
        )
        return (prompt_out,)

    def write_suffix(index, after):
        nonlocal suffix_out
        start, skip, size, a, b, relay = runs[index]
        suffix_out = suffix_outputs(
            start, tables, relay.final, relay.other, *made[index], gain, suffix_out, width, after
        )
        return (suffix_out,)

    last = make(0, last)
    last = make(1, last)
    for index in range(total + 1):
        jobs = []
        if index < total:
            jobs.append(runs[index][5].prefix_job())
        if index:
            jobs.append(runs[index - 1][5].final_job())
        results = run_steps(jobs, half, last)
        if index < total:
            prefix = results.pop(0)
            runs[index][5].cross(prefix)
            last = (prefix,)
        if index:
            last = (results[0][0],)
            runs[index - 1][5].spread(results.pop(0))
        last = make(index + 2, last)
        if index >= 2:
            relay = runs[index - 2][5]
            relay.settle(last)
            last = write_prompt(index - 2, (relay.final,))
            last = write_suffix(index - 2, last)
    relay = runs[total - 1][5]
    relay.settle(last)
    last = write_prompt(total - 1, (relay.final,))
    write_suffix(total - 1, last)
    return (prompt_out, suffix_out)


def solution(mesh):
    return jax.shard_map(
        local,
        mesh=mesh,
        in_specs=(
            P(("groups", "prompt"), "seq", "head"),
            P(("groups", "prompt"), "seq", "head"),
            P(("groups", "prompt"), "seq", "head"),
            P(("groups", "prompt"), "head", "seq"),
            P(("groups", "prompt"), "head", "seq"),
            P(("groups", "seq", "prompt"), None, "head"),
            P(("groups", "seq", "prompt"), None, "head"),
            P(("groups", "seq", "prompt"), None, "head"),
            P(("groups", "seq", "prompt"), "head", None),
            P(("groups", "seq", "prompt"), "head", None),
            P(),
            P("groups"),
            P("groups"),
            P("groups"),
        ),
        out_specs=(
            P(("groups", "prompt"), "seq", "head"),
            P(("groups", "seq", "prompt"), None, "head"),
        ),
        check_vma=False,
    )
```

```python
import functools
import math

import jax
import jax.numpy as jnp
from jax import lax
from jax.experimental import pallas as pl
from jax.experimental.pallas import tpu as pltpu
from jax.sharding import PartitionSpec as P

DK = 128
DV = 128
CH = 128
W2 = 2 * DV
EPS_NORM = 1e-06
HIGH = lax.Precision.HIGHEST
SCOPED = 24 * 1024 * 1024


def mm(left, right):
    return lax.dot_general(left, right, (((1,), (0,)), ((), ())), preferred_element_type=jnp.float32)


def diag2(pair):
    zero = jnp.zeros((pair.shape[0], DV), pair.dtype)
    top = jnp.concatenate([pair[:, :DV], zero], axis=1)
    low = jnp.concatenate([zero, pair[:, DV:]], axis=1)
    return jnp.concatenate([top, low], axis=0)


def low16(value):
    return value.astype(jnp.bfloat16)


def halves(value):
    high = low16(value)
    return high, low16(value - high.astype(jnp.float32))


def lanes2(col_a, col_b):
    shape = (col_a.shape[0], DV)
    return jnp.concatenate(
        [jnp.broadcast_to(col_a, shape), jnp.broadcast_to(col_b, shape)], axis=1
    )


def unit_rows(vectors):
    wide = vectors.astype(jnp.float32)
    factor = lax.rsqrt(jnp.sum(wide * wide, axis=-1, keepdims=True) + EPS_NORM)
    return low16(wide * factor)


def apply_pair(transfer, state, offset):
    t_hi, t_lo = halves(transfer)
    s_hi, s_lo = halves(state)
    hi = diag2(s_hi)
    return mm(t_hi, hi) + mm(t_lo, hi) + mm(t_hi, diag2(s_lo)) + offset


def gate_tables(decay):
    rows = lax.broadcasted_iota(jnp.int32, (CH, CH), 0)
    cols = lax.broadcasted_iota(jnp.int32, (CH, CH), 1)
    upper = jnp.where(rows <= cols, 1.0, 0.0).astype(jnp.float32)
    cum = lax.dot_general(
        decay, upper, (((1,), (0,)), ((), ())), precision=HIGH, preferred_element_type=jnp.float32
    )
    return cum, cum.T


def chunk_terms(chains):
    rows = lax.broadcasted_iota(jnp.int32, (CH, W2), 0)
    cols = jnp.bitwise_and(lax.broadcasted_iota(jnp.int32, (CH, W2), 1), CH - 1)
    causal = rows >= cols
    eye = jnp.where(rows == cols, 1.0, 0.0).astype(jnp.float32)
    eye16 = low16(eye)
    apart = jnp.bitwise_xor(rows, cols)
    strict = rows > cols
    masks = [
        low16(jnp.where(strict & (apart >= low) & (apart < high), -1.0, 0.0))
        for low, high in ((1, 8), (8, 32), (32, CH))
    ]

    heads = []
    for q, k, v, beta, cum_r, cum_c in chains:
        qn = unit_rows(q)
        kn = unit_rows(k)
        heads.append((qn, kn, low16(kn.astype(jnp.float32).T)))
    grams = [mm(jnp.concatenate([kn, qn], axis=0), kt) for qn, kn, kt in heads]
    lows, lefts, grows = [], [], []
    for (q, k, v, beta, cum_r, cum_c), (qn, kn, kt), gram in zip(chains, heads, grams):
        kk = gram[:CH]
        qk = gram[CH:]
        bcast = lanes2(cum_c[:, 0:1], cum_c[:, 1:2])
        row = jnp.concatenate([cum_r[0:1], cum_r[1:2]], axis=1)
        gate = jnp.concatenate([beta[0:1], beta[1:2]], axis=1)
        scaled = jnp.exp(jnp.where(causal, bcast - row, -1e30)) * gate
        lows.append(low16(scaled * jnp.concatenate([kk, kk], axis=1)))
        attn = scaled * jnp.concatenate([qk, qk], axis=1)
        last = jnp.concatenate([cum_r[0:1, CH - 1 :], cum_r[1:2, CH - 1 :]], axis=0)
        last = jnp.concatenate(
            [jnp.broadcast_to(last[0:1], (1, DV)), jnp.broadcast_to(last[1:2], (1, DV))], axis=1
        )
        tail = jnp.exp(last - row) * gate
        ktf = kt.astype(jnp.float32)
        lefts.append(halves(jnp.concatenate([attn, jnp.concatenate([ktf, ktf], axis=1) * tail], axis=0)))
        grows.append((jnp.exp(bcast), jnp.exp(row), jnp.exp(last)))
    nil = [low * masks[0] for low in lows]
    sq = [low16(mm(n, diag2(n))) for n in nil]
    fourth = [low16(mm(s, diag2(s))) for s in sq]
    inv = [low16(mm(eye16 + n, diag2(eye16 + s))) for n, s in zip(nil, sq)]
    inv = [low16(mm(i, diag2(eye16 + f))) for i, f in zip(inv, fourth)]
    for mask in masks[1:]:
        x = [low16(mm(i, diag2(low * mask))) for i, low in zip(inv, lows)]
        y = [low16(mm(eye16 + t, diag2(i))) for t, i in zip(x, inv)]
        z = [low16(mm(t, diag2(t))) for t in x]
        full = [mm(eye16 + t, diag2(i)) for t, i in zip(z, y)]
        inv = [low16(f) for f in full]
    ws = [
        low16(mm(low16(f * grow[1]), diag2(jnp.concatenate([kn, kn], axis=1))))
        for f, grow, (qn, kn, kt) in zip(full, grows, heads)
    ]
    us = [halves(mm(i, diag2(chain[2]))) for i, chain in zip(inv, chains)]
    by_w = [mm(left, diag2(w)) for (left, rest), w in zip(lefts, ws)]
    by_u = []
    for (left, rest), (u_hi, u_lo) in zip(lefts, us):
        hi = diag2(u_hi)
        by_u.append(mm(left, hi) + mm(rest, hi) + mm(left, diag2(u_lo)))
    out = []
    for (qn, kn, kt), grow, bw, bu in zip(heads, grows, by_w, by_u):
        qf = qn.astype(jnp.float32)
        a = jnp.concatenate([qf, qf], axis=1) * grow[0] - bw[:CH]
        out.append((a, bu[:CH], eye * grow[2] - bw[CH:], bu[CH:]))
    return out


def read_chains(pairs, heads, at, q_ref, k_ref, v_ref, beta_ref, decay_ref, slot, skip=0):
    beta = beta_ref[slot, heads, at]
    cum_r, cum_c = gate_tables(decay_ref[slot, heads, at])
    return [
        (
            q_ref[slot, at, (skip + p) * DK : (skip + p + 1) * DK],
            k_ref[slot, at, (skip + p) * DK : (skip + p + 1) * DK],
            v_ref[slot, at, (skip + p) * W2 : (skip + p + 1) * W2],
            beta[2 * p : 2 * p + 2],
            cum_r[2 * p : 2 * p + 2],
            cum_c[:, 2 * p : 2 * p + 2],
        )
        for p in range(pairs)
    ]


def window(first, pairs):
    return math.gcd(first, pairs) if first else pairs


def lane_specs(arrays, first, pairs, width):
    wide = window(first, pairs)
    specs, args = [], []
    for part in range(first, first + pairs, wide):
        specs.append(
            pl.BlockSpec(arrays.shape[:2] + (wide * width,), lambda i, at=part // wide: (0, 0, at))
        )
        args.append(arrays)
    return specs, args, wide


ANY = pl.BlockSpec(memory_space=pl.ANY)
WHOLE = pl.BlockSpec(memory_space=pltpu.VMEM)


SHORT = pl.CostEstimate(flops=1, transcendentals=0, bytes_accessed=1)


def near(value):
    return pltpu.with_memory_space_constraint(value, pltpu.VMEM)


def away(value):
    return pltpu.with_memory_space_constraint(value, pltpu.HBM)


class Spans:
    def __init__(self, refs, wide, width):
        self.refs, self.size, self.width = refs, wide * width, width

    def __getitem__(self, key):
        lanes = key[-1]
        part, at = divmod(lanes.start, self.size)
        return self.refs[part][key[:-1] + (slice(at, at + lanes.stop - lanes.start),)]


def places_of(sizes):
    return [(run, at) for run, size in enumerate(sizes) for at in range(size)]


def prompt_kernel(first, sizes, wide, count, *refs):
    pairs = sum(sizes)
    q_ref = Spans(refs[:count], wide, DK)
    k_ref = Spans(refs[count : 2 * count], wide, DK)
    v_ref = Spans(refs[2 * count : 3 * count], wide, W2)
    beta_ref, decay_ref = refs[3 * count : 3 * count + 2]
    outs = refs[len(refs) - 2 - len(sizes) :]
    heads = slice(2 * first, 2 * (first + pairs))
    chains = read_chains(
        pairs, heads, slice(0, CH), q_ref, k_ref, v_ref, beta_ref, decay_ref, 0
    )
    places = places_of(sizes)
    for p, (a, b, transfer, offset) in enumerate(chunk_terms(chains)):
        outs[-2][:, p * W2 : (p + 1) * W2] = low16(a)
        outs[-1][:, p * W2 : (p + 1) * W2] = low16(b)
        chunk, at = places[p]
        outs[chunk][0, at] = transfer
        outs[chunk][1, at] = offset


def prompt_terms(first, sizes, q, k, v, beta, decay, after=()):
    pairs = sum(sizes)
    q_specs, q_args, wide = lane_specs(q, first, pairs, DK)
    k_specs, k_args, wide = lane_specs(k, first, pairs, DK)
    v_specs, v_args, wide = lane_specs(v, first, pairs, W2)
    *tos, a, b = pl.pallas_call(
        functools.partial(prompt_kernel, first, sizes, wide, len(q_args)),
        grid=(1,),
        in_specs=q_specs
        + k_specs
        + v_specs
        + [
            pl.BlockSpec(beta.shape, lambda i: (0, 0, 0)),
            pl.BlockSpec(decay.shape, lambda i: (0, 0, 0)),
        ]
        + [ANY] * len(after),
        out_specs=[WHOLE] * (len(sizes) + 2),
        out_shape=[pltpu.VMEM((2, size, DK, W2), jnp.float32) for size in sizes]
        + [pltpu.VMEM((CH, pairs * W2), jnp.bfloat16)] * 2,
        compiler_params=pltpu.CompilerParams(vmem_limit_bytes=SCOPED),
        cost_estimate=SHORT,
        name="prompt_terms",
    )(*[away(value) for value in (*q_args, *k_args, *v_args, beta, decay)], *after)
    return tos, a, b


def suffix_kernel(first, unit, q_ref, k_ref, v_ref, beta_ref, decay_ref, *refs):
    a_ref, b_ref = refs[-2:]
    slots, tokens = q_ref.shape[:2]
    spans = tokens // CH
    heads = slice(2 * first, 2 * (first + unit))
    chains = []
    for slot in range(slots):
        for s in range(spans):
            at = slice(s * CH, (s + 1) * CH)
            chains += read_chains(
                unit, heads, at, q_ref, k_ref, v_ref, beta_ref, decay_ref, slot, first
            )
    terms = chunk_terms(chains)
    for slot in range(slots):
        for p in range(unit):
            lanes = slice(p * W2, (p + 1) * W2)
            a, b, transfer, offset = terms[slot * spans * unit + p]
            a_ref[slot, 0:CH, lanes] = low16(a)
            b_ref[slot, 0:CH, lanes] = low16(b)
            for s in range(1, spans):
                a, b, t_next, o_next = terms[(slot * spans + s) * unit + p]
                a16 = low16(a)
                at = slice(s * CH, (s + 1) * CH)
                d_t = diag2(low16(transfer))
                d_o = diag2(low16(offset))
                a_ref[slot, at, lanes] = low16(mm(a16, d_t))
                b_ref[slot, at, lanes] = low16(mm(a16, d_o) + b)
                if s + 1 < spans:
                    t16 = low16(t_next)
                    transfer, offset = mm(t16, d_t), mm(t16, d_o) + o_next


def suffix_terms(first, unit, q, k, v, beta, decay, after=()):
    slots, tokens = q.shape[0], q.shape[1]
    return pl.pallas_call(
        functools.partial(suffix_kernel, first, unit),
        in_specs=[WHOLE] * 5 + [ANY] * len(after),
        out_specs=[WHOLE] * 2,
        out_shape=[pltpu.VMEM((slots, tokens, unit * W2), jnp.bfloat16)] * 2,
        compiler_params=pltpu.CompilerParams(vmem_limit_bytes=SCOPED),
        cost_estimate=SHORT,
        name="suffix_terms",
    )(near(q), near(k), near(v), near(beta), near(decay), *after)


def step_kernel(kinds, half, *refs):
    here = lax.axis_index("seq")
    refs = list(refs)
    counts = {"step": 2, "twice": 3}
    inputs = []
    for kind in kinds:
        inputs.append([refs.pop(0) for _ in range(counts[kind])])
    outs = refs[len(refs) - sum(2 if kind == "twice" else 1 for kind in kinds) :]
    for kind, ins in zip(kinds, inputs):
        if kind == "step":
            out = outs.pop(0)

            @pl.when(here < half)
            def _(ins=ins, out=out):
                for p in range(out.shape[0]):
                    out[p] = apply_pair(ins[0][0, p], ins[1][1, p], ins[0][1, p])

        else:
            out, final = outs.pop(0), outs.pop(0)

            @pl.when(here == half)
            def _(ins=ins, out=out, final=final):
                for p in range(out.shape[0]):
                    state = apply_pair(ins[0][0, p], ins[2][p], ins[0][1, p])
                    out[p] = state
                    final[p] = apply_pair(ins[1][0, p], state, ins[1][1, p])


def run_steps(jobs, half, after=()):
    kinds = tuple(job[0] for job in jobs)
    args, shapes = [], []
    for kind, *ins in jobs:
        args += [near(value) for value in ins]
        shape = pltpu.VMEM(ins[0].shape[1:], jnp.float32)
        shapes += [shape] * (2 if kind == "twice" else 1)
    outs = pl.pallas_call(
        functools.partial(step_kernel, kinds, half),
        in_specs=[WHOLE] * len(args) + [ANY] * len(after),
        out_specs=[WHOLE] * len(shapes),
        out_shape=shapes,
        compiler_params=pltpu.CompilerParams(vmem_limit_bytes=SCOPED),
        cost_estimate=SHORT,
        name="state_steps",
    )(*args, *after)
    outs = list(outs)
    results = []
    for kind in kinds:
        if kind == "twice":
            results.append((outs.pop(0), outs.pop(0)))
        else:
            results.append(outs.pop(0))
    return results


def settle_kernel(half, sizes, *refs):
    here = lax.axis_index("seq")
    out_ref = refs[-1]
    at = 0
    for run, size in enumerate(sizes):
        to_ref, right_ref, *finals = refs[run * (half + 3) : (run + 1) * (half + 3)]
        for d in range(half + 1):

            @pl.when(here == d)
            def _(at=at, size=size, source=finals[d]):
                out_ref[at : at + size] = source[...]

        @pl.when(here > half)
        def _(at=at, size=size, to_ref=to_ref, right_ref=right_ref):
            for p in range(size):
                out_ref[at + p] = apply_pair(to_ref[0, p], right_ref[p], to_ref[1, p])

        at += size


def settle(runs, half, after=()):
    sizes = [to.shape[1] for to, right, lefts, mid in runs]
    args = [x for to, right, lefts, mid in runs for x in (to, right, *lefts, mid)]
    return pl.pallas_call(
        functools.partial(settle_kernel, half, sizes),
        in_specs=[WHOLE] * len(args) + [ANY] * len(after),
        out_specs=WHOLE,
        out_shape=pltpu.VMEM((sum(sizes), DK, W2), jnp.float32),
        compiler_params=pltpu.CompilerParams(vmem_limit_bytes=SCOPED),
        cost_estimate=SHORT,
        name="settle",
    )(*[near(value) for value in args], *after)


def finish(a, state, b, gain2):
    raw = mm(a, diag2(low16(state))) + b.astype(jnp.float32)
    share = diag2(jnp.full((DV, W2), 1.0 / DV, jnp.bfloat16))
    return raw * lax.rsqrt(mm(low16(raw * raw), share) + EPS_NORM) * gain2


def suffix_out_kernel(sizes, slots, n_prompt, *refs):
    sb_ref, bl_ref, bp_ref, own_ref, other_ref, gain_ref = refs[:6]
    out_ref = refs[-1]
    me = lax.axis_index("prompt")
    rank = lax.axis_index("seq") * n_prompt + me
    slot = pl.program_id(0)
    branch = sb_ref[rank * slots + slot]
    length = bl_ref[branch]
    mine = bp_ref[branch] == me
    gain = gain_ref[...]
    gain2 = jnp.concatenate([gain, gain], axis=1)
    tokens = out_ref.shape[1]
    live = lax.broadcasted_iota(jnp.int32, (tokens, W2), 0) < length
    for p, (run, at) in enumerate(places_of(sizes)):
        source = slice(at * W2, (at + 1) * W2)
        a_ref, b_ref = refs[6 + 2 * run : 8 + 2 * run]
        state = jnp.where(mine, own_ref[p], other_ref[p])
        out = finish(a_ref[slot, :, source], state, b_ref[slot, :, source], gain2)
        out_ref[0, :, p * W2 : (p + 1) * W2] = low16(jnp.where(live, out, 0.0))


def suffix_outputs(first, tables, own, other, terms, gain, so_far, width, after=()):
    slots, tokens, _ = terms[0][0].shape
    sizes = [a.shape[2] // W2 for a, b in terms]
    pairs = sum(sizes)
    at = first // pairs
    args = [own, other, gain] + [x for pair in terms for x in pair]
    in_specs = [pl.BlockSpec(memory_space=pltpu.SMEM)] * 3 + [WHOLE] * len(args)
    args = list(tables) + [near(value) for value in args]
    aliases = {}
    if so_far is not None:
        aliases = {len(args): 0}
        in_specs.append(ANY)
        args.append(away(so_far))
    return pl.pallas_call(
        functools.partial(suffix_out_kernel, sizes, slots, lax.axis_size("prompt")),
        grid=(slots,),
        in_specs=in_specs + [ANY] * len(after),
        out_specs=pl.BlockSpec((1, tokens, pairs * W2), lambda i: (i, 0, at)),
        out_shape=pltpu.HBM((slots, tokens, width), jnp.bfloat16),
        input_output_aliases=aliases,
        compiler_params=pltpu.CompilerParams(vmem_limit_bytes=SCOPED),
        cost_estimate=SHORT,
        name="suffix_out",
    )(*args, *after)


def prompt_out_kernel(half, calls, sizes, *refs):
    here = lax.axis_index("seq")
    came = refs[: 3 * len(sizes)]
    terms = refs[len(came) : len(came) + 2 * len(calls)]
    gain_ref = refs[len(came) + len(terms)]
    out_ref, state_ref = refs[-2:]
    at = 0
    for run, size in enumerate(sizes):
        far_ref, mid_ref, right_ref = came[3 * run : 3 * run + 3]

        @pl.when(here < half)
        def _(at=at, size=size, far_ref=far_ref):
            state_ref[at : at + size] = far_ref[1]

        @pl.when(here == half)
        def _(at=at, size=size, mid_ref=mid_ref):
            state_ref[at : at + size] = mid_ref[...]

        @pl.when(here > half)
        def _(at=at, size=size, right_ref=right_ref):
            state_ref[at : at + size] = right_ref[...]

        at += size
    gain = gain_ref[...]
    gain2 = jnp.concatenate([gain, gain], axis=1)
    for p, (call, at) in enumerate(places_of(calls)):
        source = slice(at * W2, (at + 1) * W2)
        a, b = terms[2 * call][:, source], terms[2 * call + 1][:, source]
        out_ref[0, :, p * W2 : (p + 1) * W2] = low16(finish(a, state_ref[p], b, gain2))


def prompt_outputs(half, came, terms, gain, width, after=()):
    pairs = width // W2
    calls = [a.shape[1] // W2 for a, b in terms]
    sizes = [mid.shape[0] for far, mid, right in came]
    args = [x for run in came for x in run] + [x for pair in terms for x in pair] + [gain]
    return pl.pallas_call(
        functools.partial(prompt_out_kernel, half, calls, sizes),
        grid=(1,),
        in_specs=[WHOLE] * len(args) + [ANY] * len(after),
        out_specs=pl.BlockSpec((1, CH, width), lambda i: (0, 0, 0)),
        out_shape=pltpu.HBM((1, CH, width), jnp.bfloat16),
        scratch_shapes=[pltpu.VMEM((pairs, DK, W2), jnp.float32)],
        compiler_params=pltpu.CompilerParams(vmem_limit_bytes=SCOPED),
        cost_estimate=SHORT,
        name="prompt_out",
    )(*[near(value) for value in args], *after)


def pair_product(left, right):
    pairs = left.shape[0]
    left = left.reshape(pairs, DK, 2, DK)
    right = right.reshape(pairs, DK, 2, DV)
    return jnp.einsum("pihj,pjhv->pihv", left, right, precision=HIGH).reshape(pairs, DK, W2)


class Relay:
    def __init__(self, to):
        self.to = to
        self.count = lax.axis_size("seq")
        self.half = self.count // 2
        self.here = lax.axis_index("seq")

    def open(self):
        count, half = self.count, self.half
        sending, far = self.to, None
        for j in range(half - 1):
            arrived = lax.ppermute(sending, "seq", [(j, j + 1), (count - 1 - j, count - 2 - j)])
            far = arrived if far is None else far + arrived
            if j + 2 < half:
                prefix = pair_product(self.to[0], arrived[1]) + self.to[1]
                joined = jnp.stack(
                    [
                        pair_product(arrived[0], self.to[0]),
                        pair_product(arrived[0], self.to[1]) + arrived[1],
                    ]
                )
                sending = jnp.where(self.here < half, jnp.stack([prefix, prefix]), joined)
        self.far = far

    def prefix_job(self):
        return ("step", self.to, self.far)

    def cross(self, prefix):
        self.mid = lax.ppermute(prefix, "seq", [(self.half - 1, self.half)])

    def final_job(self):
        return ("twice", self.to, self.far, self.mid)

    def spread(self, result):
        state, self.final_mid = result
        half, count = self.half, self.count
        self.lefts, passed = [], self.final_mid
        for d in range(half - 1, -1, -1):
            passed = lax.ppermute(passed, "seq", [(d + 1, d)])
            self.lefts.insert(0, passed)
        right = None
        for j in range(half - 1):
            arrived = lax.ppermute(state, "seq", [(half + j, half + j + 1)])
            right = arrived if right is None else right + arrived
            if j + 2 < half:
                state = pair_product(self.to[0], arrived) + self.to[1]
        self.right = right


def settle_runs(relays, after):
    half, count, here = relays[0].half, relays[0].count, relays[0].here
    final = settle([(r.to, r.right, r.lefts, r.final_mid) for r in relays], half, after)
    if half > 2:
        inner = (here > half) & (here < count - 1)
        far = jnp.concatenate([r.far for r in relays], axis=1)
        final = jnp.where(inner, pair_product(far[0], final) + far[1], final)
    prompts = lax.axis_size("prompt")
    other = lax.ppermute(final, "prompt", [(i, (i + 1) % prompts) for i in range(prompts)])
    return final, other


def plan_of(pairs):
    if pairs % 4:
        return [[1]] * pairs, [1] * pairs
    unit = pairs // 4
    return [[unit], [unit, unit, unit]], [3, 1]


def local(
    prompt_queries,
    prompt_keys,
    prompt_values,
    prompt_beta,
    prompt_decay,
    suffix_queries,
    suffix_keys,
    suffix_values,
    suffix_beta,
    suffix_decay,
    norm_gain,
    slot_branch,
    branch_length,
    branch_prompt,
):
    gain = norm_gain.reshape(1, DV)
    tables = (slot_branch, branch_length, branch_prompt)
    width = prompt_values.shape[2]
    prompt_in = (prompt_queries, prompt_keys, prompt_values, prompt_beta, prompt_decay)
    suffix_in = (suffix_queries, suffix_keys, suffix_values, suffix_beta, suffix_decay)
    half = lax.axis_size("seq") // 2

    calls, ends = plan_of(width // W2)
    relays, firsts, terms = [], [], []
    first, last = 0, ()
    for sizes in calls:
        tos, a, b = prompt_terms(first, sizes, *prompt_in, after=last)
        last = (near(a),)
        terms.append((a, b))
        for to, size in zip(tos, sizes):
            relay = Relay(to)
            relay.open()
            relays.append(relay)
            firsts.append(first)
            first += size
    total = len(relays)
    made = []

    def make(after):
        if len(made) == total:
            return after
        index = len(made)
        size = relays[index].to.shape[1]
        made.append(suffix_terms(firsts[index], size, *suffix_in, after=after))
        return (near(made[index][0]),)

    def landed(index):
        return tuple(
            near(relays[index - 2 - j].lefts[half - 1 - j])
            for j in range(half)
            if 0 <= index - 2 - j < total
        )

    last = make(make(last))
    for index in range(total + 2):
        if index < total:
            (prefix,) = run_steps([relays[index].prefix_job()], half, last)
            relays[index].cross(prefix)
            last = (near(prefix),)
        if 0 < index <= total:
            (result,) = run_steps([relays[index - 1].final_job()], half, last)
            relays[index - 1].spread(result)
            last = (near(result[0]),)
        last = make(last) + landed(index)
    came = [(relay.far, relay.mid, relay.right) for relay in relays]
    prompt_out = prompt_outputs(half, came, terms, gain, width, last)
    last = (away(prompt_out),)
    suffix_out = None
    index = 0
    for runs in ends:
        own, other = settle_runs(relays[index : index + runs], last)
        suffix_out = suffix_outputs(
            firsts[index], tables, own, other, made[index : index + runs], gain, suffix_out, width
        )
        last = (away(suffix_out),)
        index += runs
    return (prompt_out, suffix_out)


def solution(mesh):
    return jax.shard_map(
        local,
        mesh=mesh,
        in_specs=(
            P(("groups", "prompt"), "seq", "head"),
            P(("groups", "prompt"), "seq", "head"),
            P(("groups", "prompt"), "seq", "head"),
            P(("groups", "prompt"), "head", "seq"),
            P(("groups", "prompt"), "head", "seq"),
            P(("groups", "seq", "prompt"), None, "head"),
            P(("groups", "seq", "prompt"), None, "head"),
            P(("groups", "seq", "prompt"), None, "head"),
            P(("groups", "seq", "prompt"), "head", None),
            P(("groups", "seq", "prompt"), "head", None),
            P(),
            P("groups"),
            P("groups"),
            P("groups"),
        ),
        out_specs=(
            P(("groups", "prompt"), "seq", "head"),
            P(("groups", "seq", "prompt"), None, "head"),
        ),
        check_vma=False,
    )
```

```python
import functools
import math

import jax
import jax.numpy as jnp
from jax import lax
from jax.experimental import pallas as pl
from jax.experimental.pallas import tpu as pltpu
from jax.sharding import PartitionSpec as P

DK = 128
DV = 128
CH = 128
W2 = 2 * DV
EPS_NORM = 1e-06
HIGH = lax.Precision.HIGHEST
SCOPED = 24 * 1024 * 1024


def mm(left, right):
    return lax.dot_general(left, right, (((1,), (0,)), ((), ())), preferred_element_type=jnp.float32)


def diag2(pair):
    zero = jnp.zeros((pair.shape[0], DV), pair.dtype)
    top = jnp.concatenate([pair[:, :DV], zero], axis=1)
    low = jnp.concatenate([zero, pair[:, DV:]], axis=1)
    return jnp.concatenate([top, low], axis=0)


def low16(value):
    return value.astype(jnp.bfloat16)


def halves(value):
    high = low16(value)
    return high, low16(value - high.astype(jnp.float32))


def lanes2(col_a, col_b):
    shape = (col_a.shape[0], DV)
    return jnp.concatenate(
        [jnp.broadcast_to(col_a, shape), jnp.broadcast_to(col_b, shape)], axis=1
    )


def unit_rows(vectors):
    wide = vectors.astype(jnp.float32)
    factor = lax.rsqrt(jnp.sum(wide * wide, axis=-1, keepdims=True) + EPS_NORM)
    return low16(wide * factor)


def apply_pair(transfer, state, offset):
    t_hi, t_lo = halves(transfer)
    s_hi, s_lo = halves(state)
    hi = diag2(s_hi)
    return mm(t_hi, hi) + mm(t_lo, hi) + mm(t_hi, diag2(s_lo)) + offset


def gate_tables(decay):
    rows = lax.broadcasted_iota(jnp.int32, (CH, CH), 0)
    cols = lax.broadcasted_iota(jnp.int32, (CH, CH), 1)
    upper = jnp.where(rows <= cols, 1.0, 0.0).astype(jnp.float32)
    cum = lax.dot_general(
        decay, upper, (((1,), (0,)), ((), ())), precision=HIGH, preferred_element_type=jnp.float32
    )
    return cum, cum.T


def chunk_terms(chains):
    rows = lax.broadcasted_iota(jnp.int32, (CH, W2), 0)
    cols = jnp.bitwise_and(lax.broadcasted_iota(jnp.int32, (CH, W2), 1), CH - 1)
    causal = rows >= cols
    eye = jnp.where(rows == cols, 1.0, 0.0).astype(jnp.float32)
    eye16 = low16(eye)
    apart = jnp.bitwise_xor(rows, cols)
    strict = rows > cols
    masks = [
        low16(jnp.where(strict & (apart >= low) & (apart < high), -1.0, 0.0))
        for low, high in ((1, 8), (8, 32), (32, CH))
    ]

    heads = []
    for q, k, v, beta, cum_r, cum_c, ends in chains:
        qn = unit_rows(q)
        kn = unit_rows(k)
        heads.append((qn, kn, low16(kn.astype(jnp.float32).T)))
    grams = []
    for one, two in zip(heads[::2], heads[1::2]):
        rows_of = jnp.concatenate(
            [jnp.concatenate(one[1::-1], axis=0), jnp.concatenate(two[1::-1], axis=0)], axis=1
        )
        both = mm(rows_of, diag2(jnp.concatenate([one[2], two[2]], axis=1)))
        grams += [both[:, :DK], both[:, DK:]]
    if len(heads) % 2:
        qn, kn, kt = heads[-1]
        grams.append(mm(jnp.concatenate([kn, qn], axis=0), kt))
    lows, lefts, grows = [], [], []
    for (q, k, v, beta, cum_r, cum_c, ends), (qn, kn, kt), gram in zip(chains, heads, grams):
        kk = gram[:CH]
        qk = gram[CH:]
        bcast = lanes2(cum_c[:, 0:1], cum_c[:, 1:2])
        row = jnp.concatenate([cum_r[0:1], cum_r[1:2]], axis=1)
        gate = jnp.concatenate([beta[0:1], beta[1:2]], axis=1)
        scaled = jnp.exp(jnp.where(causal, bcast - row, -1e30)) * gate
        lows.append(low16(scaled * jnp.concatenate([kk, kk], axis=1)))
        attn = scaled * jnp.concatenate([qk, qk], axis=1)
        last = jnp.concatenate([cum_r[0:1, CH - 1 :], cum_r[1:2, CH - 1 :]], axis=0)
        last = jnp.concatenate(
            [jnp.broadcast_to(last[0:1], (1, DV)), jnp.broadcast_to(last[1:2], (1, DV))], axis=1
        )
        tail = jnp.exp(last - row) * gate
        ktf = kt.astype(jnp.float32)
        if ends:
            lefts.append(halves(attn))
        else:
            tail_k = jnp.concatenate([ktf, ktf], axis=1) * tail
            lefts.append(halves(jnp.concatenate([attn, tail_k], axis=0)))
        grows.append((jnp.exp(bcast), jnp.exp(row), jnp.exp(last)))
    nil = [low * masks[0] for low in lows]
    sq = [low16(mm(n, diag2(n))) for n in nil]
    fourth = [low16(mm(s, diag2(s))) for s in sq]
    inv = [low16(mm(eye16 + n, diag2(eye16 + s))) for n, s in zip(nil, sq)]
    inv = [low16(mm(i, diag2(eye16 + f))) for i, f in zip(inv, fourth)]
    for mask in masks[1:]:
        x = [low16(mm(i, diag2(low * mask))) for i, low in zip(inv, lows)]
        y = [low16(mm(eye16 + t, diag2(i))) for t, i in zip(x, inv)]
        z = [low16(mm(t, diag2(t))) for t in x]
        full = [mm(eye16 + t, diag2(i)) for t, i in zip(z, y)]
        inv = [low16(f) for f in full]
    ws = [
        low16(mm(low16(f * grow[1]), diag2(jnp.concatenate([kn, kn], axis=1))))
        for f, grow, (qn, kn, kt) in zip(full, grows, heads)
    ]
    us = [halves(mm(i, diag2(chain[2]))) for i, chain in zip(inv, chains)]
    by_w = [mm(left, diag2(w)) for (left, rest), w in zip(lefts, ws)]
    by_u = []
    for (left, rest), (u_hi, u_lo) in zip(lefts, us):
        hi = diag2(u_hi)
        by_u.append(mm(left, hi) + mm(rest, hi) + mm(left, diag2(u_lo)))
    out = []
    for (qn, kn, kt), grow, bw, bu in zip(heads, grows, by_w, by_u):
        qf = qn.astype(jnp.float32)
        a = jnp.concatenate([qf, qf], axis=1) * grow[0] - bw[:CH]
        if bw.shape[0] == CH:
            out.append((a, bu, None, None))
        else:
            out.append((a, bu[:CH], eye * grow[2] - bw[CH:], bu[CH:]))
    return out


def read_chains(pairs, heads, at, q_ref, k_ref, v_ref, beta_ref, decay_ref, slot, skip=0, ends=False):
    beta = beta_ref[slot, heads, at]
    cum_r, cum_c = gate_tables(decay_ref[slot, heads, at])
    return [
        (
            q_ref[slot, at, (skip + p) * DK : (skip + p + 1) * DK],
            k_ref[slot, at, (skip + p) * DK : (skip + p + 1) * DK],
            v_ref[slot, at, (skip + p) * W2 : (skip + p + 1) * W2],
            beta[2 * p : 2 * p + 2],
            cum_r[2 * p : 2 * p + 2],
            cum_c[:, 2 * p : 2 * p + 2],
            ends,
        )
        for p in range(pairs)
    ]


def window(first, pairs):
    return math.gcd(first, pairs) if first else pairs


def lane_specs(arrays, first, pairs, width):
    wide = window(first, pairs)
    specs, args = [], []
    for part in range(first, first + pairs, wide):
        specs.append(
            pl.BlockSpec(arrays.shape[:2] + (wide * width,), lambda i, at=part // wide: (0, 0, at))
        )
        args.append(arrays)
    return specs, args, wide


ANY = pl.BlockSpec(memory_space=pl.ANY)
WHOLE = pl.BlockSpec(memory_space=pltpu.VMEM)


SHORT = pl.CostEstimate(flops=1, transcendentals=0, bytes_accessed=1)


def near(value):
    return pltpu.with_memory_space_constraint(value, pltpu.VMEM)


def away(value):
    return pltpu.with_memory_space_constraint(value, pltpu.HBM)


class Spans:
    def __init__(self, refs, wide, width):
        self.refs, self.size, self.width = refs, wide * width, width

    def __getitem__(self, key):
        lanes = key[-1]
        part, at = divmod(lanes.start, self.size)
        return self.refs[part][key[:-1] + (slice(at, at + lanes.stop - lanes.start),)]


def places_of(sizes):
    return [(run, at) for run, size in enumerate(sizes) for at in range(size)]


def prompt_kernel(first, sizes, wide, count, *refs):
    pairs = sum(sizes)
    q_ref = Spans(refs[:count], wide, DK)
    k_ref = Spans(refs[count : 2 * count], wide, DK)
    v_ref = Spans(refs[2 * count : 3 * count], wide, W2)
    beta_ref, decay_ref = refs[3 * count : 3 * count + 2]
    *both, a_ref, b_ref = refs[len(refs) - 2 - len(sizes) :]
    heads = slice(2 * first, 2 * (first + pairs))
    chains = read_chains(
        pairs, heads, slice(0, CH), q_ref, k_ref, v_ref, beta_ref, decay_ref, 0
    )
    places = places_of(sizes)
    for p, (a, b, transfer, offset) in enumerate(chunk_terms(chains)):
        a_ref[:, p * W2 : (p + 1) * W2] = low16(a)
        b_ref[:, p * W2 : (p + 1) * W2] = low16(b)
        run, at = places[p]
        both[run][0, at] = transfer
        both[run][1, at] = offset


def prompt_terms(first, sizes, q, k, v, beta, decay, after=()):
    pairs = sum(sizes)
    q_specs, q_args, wide = lane_specs(q, first, pairs, DK)
    k_specs, k_args, wide = lane_specs(k, first, pairs, DK)
    v_specs, v_args, wide = lane_specs(v, first, pairs, W2)
    *boths, a, b = pl.pallas_call(
        functools.partial(prompt_kernel, first, sizes, wide, len(q_args)),
        grid=(1,),
        in_specs=q_specs
        + k_specs
        + v_specs
        + [
            pl.BlockSpec(beta.shape, lambda i: (0, 0, 0)),
            pl.BlockSpec(decay.shape, lambda i: (0, 0, 0)),
        ]
        + [ANY] * len(after),
        out_specs=[WHOLE] * (len(sizes) + 2),
        out_shape=[pltpu.VMEM((2, size, DK, W2), jnp.float32) for size in sizes]
        + [pltpu.VMEM((CH, pairs * W2), jnp.bfloat16)] * 2,
        compiler_params=pltpu.CompilerParams(vmem_limit_bytes=SCOPED),
        cost_estimate=SHORT,
        name="prompt_terms",
    )(*[away(value) for value in (*q_args, *k_args, *v_args, beta, decay)], *after)
    return boths, a, b


def suffix_kernel(first, unit, q_ref, k_ref, v_ref, beta_ref, decay_ref, *refs):
    a_ref, b_ref = refs[-2:]
    slots, tokens = q_ref.shape[:2]
    spans = tokens // CH
    heads = slice(2 * first, 2 * (first + unit))
    chains = []
    for slot in range(slots):
        for s in range(spans):
            at = slice(s * CH, (s + 1) * CH)
            chains += read_chains(
                unit, heads, at, q_ref, k_ref, v_ref, beta_ref, decay_ref, slot, first, s + 1 == spans
            )
    terms = chunk_terms(chains)
    for slot in range(slots):
        for p in range(unit):
            lanes = slice(p * W2, (p + 1) * W2)
            a, b, transfer, offset = terms[slot * spans * unit + p]
            a_ref[slot, 0:CH, lanes] = low16(a)
            b_ref[slot, 0:CH, lanes] = low16(b)
            for s in range(1, spans):
                a, b, t_next, o_next = terms[(slot * spans + s) * unit + p]
                a16 = low16(a)
                at = slice(s * CH, (s + 1) * CH)
                d_t = diag2(low16(transfer))
                d_o = diag2(low16(offset))
                a_ref[slot, at, lanes] = low16(mm(a16, d_t))
                b_ref[slot, at, lanes] = low16(mm(a16, d_o) + b)
                if s + 1 < spans:
                    t16 = low16(t_next)
                    transfer, offset = mm(t16, d_t), mm(t16, d_o) + o_next


def suffix_terms(first, unit, q, k, v, beta, decay, after=()):
    slots, tokens = q.shape[0], q.shape[1]
    return pl.pallas_call(
        functools.partial(suffix_kernel, first, unit),
        in_specs=[WHOLE] * 5 + [ANY] * len(after),
        out_specs=[WHOLE] * 2,
        out_shape=[pltpu.VMEM((slots, tokens, unit * W2), jnp.bfloat16)] * 2,
        compiler_params=pltpu.CompilerParams(vmem_limit_bytes=SCOPED),
        cost_estimate=SHORT,
        name="suffix_terms",
    )(near(q), near(k), near(v), near(beta), near(decay), *after)


def call_near(kernel, shapes, name, args, after=(), scratch=()):
    out = pl.pallas_call(
        kernel,
        in_specs=[WHOLE] * len(args) + [ANY] * len(after),
        out_specs=[WHOLE] * len(shapes),
        out_shape=[pltpu.VMEM(shape, jnp.float32) for shape in shapes],
        scratch_shapes=scratch,
        compiler_params=pltpu.CompilerParams(vmem_limit_bytes=SCOPED),
        cost_estimate=SHORT,
        name=name,
    )(*[near(value) for value in args], *after)
    return list(out)


def pair_at(ref, index):
    if len(ref.shape) == 3:
        return ref[index]
    return ref[index // ref.shape[1], index % ref.shape[1]]


def pack_kernel(half, sizes, *refs):
    both_ref, out_ref = refs[len(sizes)], refs[-1]
    here = lax.axis_index("seq")

    @pl.when(here < half)
    def _():
        for p, (run, at) in enumerate(places_of(sizes)):
            out_ref[p // out_ref.shape[1], p % out_ref.shape[1]] = refs[run][1, at]

    @pl.when(here >= half)
    def _():
        out_ref[...] = both_ref[...]


def pack(half, boths, both, after):
    sizes = [other.shape[1] for other in boths]
    (out,) = call_near(
        functools.partial(pack_kernel, half, sizes), [both.shape], "pack", [*boths, both], after
    )
    return out


def part_kernel(half, skips, left_ref, state_ref, *refs):
    out_ref = refs[-1]
    here = lax.axis_index("seq")

    @pl.when(here < half)
    def _():
        out_ref[...] = left_ref[skips[0] : skips[0] + out_ref.shape[0]]

    @pl.when(here >= half)
    def _():
        out_ref[...] = state_ref[skips[1] : skips[1] + out_ref.shape[0]]


def part(half, size, left, right, after):
    (out,) = call_near(
        functools.partial(part_kernel, half, (left[1], right[1])),
        [(size, DK, W2)],
        "part",
        [left[0], right[0]],
        after,
    )
    return out


def step_kernel(user, sizes, skip, *refs):
    state_ref, out_ref = refs[len(sizes)], refs[-1]

    @pl.when(lax.axis_index("seq") == user)
    def _():
        for p, (run, at) in enumerate(places_of(sizes)):
            out_ref[p] = apply_pair(refs[run][0, at], pair_at(state_ref, skip + p), refs[run][1, at])


def step(user, boths, state, after, skip=0):
    sizes = [both.shape[1] for both in boths]
    (out,) = call_near(
        functools.partial(step_kernel, user, sizes, skip),
        [(sum(sizes), DK, W2)],
        "state_step",
        [*boths, state],
        after,
    )
    return out


def meet_kernel(user, skip, far_ref, state_ref, *refs):
    out_ref = refs[-1]

    @pl.when(lax.axis_index("seq") == user)
    def _():
        for p in range(out_ref.shape[0]):
            out_ref[p] = apply_pair(far_ref[0, p], state_ref[skip + p], far_ref[1, p])


def meet(user, far, skip, state, after):
    (out,) = call_near(
        functools.partial(meet_kernel, user, skip),
        [far.shape[1:]],
        "final_state",
        [far, state],
        after,
    )
    return out


def settle_kernel(sizes, skips, *refs):
    here = lax.axis_index("seq")
    out_ref = refs[-1]
    wide = len(skips[0])
    at = 0
    for run, size in enumerate(sizes):
        for d, skip in enumerate(skips[run]):

            @pl.when(here == d)
            def _(at=at, size=size, skip=skip, source=refs[run * wide + d]):
                out_ref[at : at + size] = source[skip : skip + size]

        at += size


def settle(runs, after):
    sizes = [size for held, size in runs]
    (out,) = call_near(
        functools.partial(settle_kernel, sizes, [[skip for x, skip in held] for held, size in runs]),
        [(sum(sizes), DK, W2)],
        "settle",
        [x for held, size in runs for x, skip in held],
        after,
    )
    return out


def slot_rows_kernel(slots, n_prompt, sb_ref, bl_ref, bp_ref, *refs):
    out_ref = refs[-1]
    me = lax.axis_index("prompt")
    rank = lax.axis_index("seq") * n_prompt + me
    for slot in range(slots):
        branch = sb_ref[rank * slots + slot]
        mine = jnp.where(bp_ref[branch] == me, 1, 0)
        out_ref[slot, 0:8] = jnp.full((8, W2), bl_ref[branch], jnp.int32)
        out_ref[slot, 8:16] = jnp.full((8, W2), mine, jnp.int32)


def slot_rows(slots, tables, after):
    return pl.pallas_call(
        functools.partial(slot_rows_kernel, slots, lax.axis_size("prompt")),
        in_specs=[pl.BlockSpec(memory_space=pltpu.SMEM)] * 3 + [ANY] * len(after),
        out_specs=WHOLE,
        out_shape=pltpu.VMEM((slots, 16, W2), jnp.int32),
        compiler_params=pltpu.CompilerParams(vmem_limit_bytes=SCOPED),
        cost_estimate=SHORT,
        name="slot_rows",
    )(*tables, *after)


def finish(a, state, b, gain2):
    raw = mm(a, diag2(low16(state))) + b.astype(jnp.float32)
    share = diag2(jnp.full((DV, W2), 1.0 / DV, jnp.bfloat16))
    return raw * lax.rsqrt(mm(low16(raw * raw), share) + EPS_NORM) * gain2


def suffix_out_kernel(sizes, *refs):
    rows_ref, own_ref, other_ref, gain_ref = refs[:4]
    out_ref = refs[-1]
    slot = pl.program_id(0)
    mine = rows_ref[slot, 8:9] == 1
    gain = gain_ref[...]
    gain2 = jnp.concatenate([gain, gain], axis=1)
    tokens = out_ref.shape[1]
    live = lax.broadcasted_iota(jnp.int32, (tokens, W2), 0) < rows_ref[slot, 0:1]
    for p, (run, at) in enumerate(places_of(sizes)):
        source = slice(at * W2, (at + 1) * W2)
        a_ref, b_ref = refs[4 + 2 * run : 6 + 2 * run]
        state = jnp.where(mine, own_ref[p], other_ref[p])
        out = finish(a_ref[slot, :, source], state, b_ref[slot, :, source], gain2)
        out_ref[0, :, p * W2 : (p + 1) * W2] = low16(jnp.where(live, out, 0.0))


def suffix_outputs(first, rows, own, other, terms, gain, so_far, width, after=()):
    slots, tokens, _ = terms[0][0].shape
    sizes = [a.shape[2] // W2 for a, b in terms]
    pairs = sum(sizes)
    at = first // pairs
    args = [rows, own, other, gain] + [x for pair in terms for x in pair]
    in_specs = [WHOLE] * len(args)
    args = [near(value) for value in args]
    aliases = {}
    if so_far is not None:
        aliases = {len(args): 0}
        in_specs.append(ANY)
        args.append(away(so_far))
    return pl.pallas_call(
        functools.partial(suffix_out_kernel, sizes),
        grid=(slots,),
        in_specs=in_specs + [ANY] * len(after),
        out_specs=pl.BlockSpec((1, tokens, pairs * W2), lambda i: (i, 0, at)),
        out_shape=pltpu.HBM((slots, tokens, width), jnp.bfloat16),
        input_output_aliases=aliases,
        compiler_params=pltpu.CompilerParams(vmem_limit_bytes=SCOPED),
        cost_estimate=SHORT,
        name="suffix_out",
    )(*args, *after)


def prompt_out_kernel(calls, hops, *refs):
    here = lax.axis_index("seq")
    refs, out_ref, state_ref = list(refs[:-2]), refs[-2], refs[-1]
    for j, sizes in enumerate(hops):
        arrived = [refs.pop(0) for _ in sizes]

        @pl.when((here == j + 1) | ((here == 0) & (j == 0)))
        def _(sizes=sizes, arrived=arrived):
            for p, (run, at) in enumerate(places_of(sizes)):
                state_ref[p] = pair_at(arrived[run], at)

    terms = [(refs.pop(0), refs.pop(0)) for _ in calls]
    gain = refs[0][...]
    gain2 = jnp.concatenate([gain, gain], axis=1)
    for p, (call, at) in enumerate(places_of(calls)):
        source = slice(at * W2, (at + 1) * W2)
        a_ref, b_ref = terms[call]
        out = finish(a_ref[:, source], state_ref[p], b_ref[:, source], gain2)
        out_ref[0, :, p * W2 : (p + 1) * W2] = low16(out)


def prompt_outputs(arrived, terms, gain, width, after=()):
    pairs = width // W2
    calls = [a.shape[1] // W2 for a, b in terms]
    hops = [[size for x, size in hop] for hop in arrived]
    args = [x for hop in arrived for x, size in hop] + [x for pair in terms for x in pair] + [gain]
    return pl.pallas_call(
        functools.partial(prompt_out_kernel, calls, hops),
        grid=(1,),
        in_specs=[WHOLE] * len(args) + [ANY] * len(after),
        out_specs=pl.BlockSpec((1, CH, width), lambda i: (0, 0, 0)),
        out_shape=pltpu.HBM((1, CH, width), jnp.bfloat16),
        scratch_shapes=[pltpu.VMEM((pairs, DK, W2), jnp.float32)],
        compiler_params=pltpu.CompilerParams(vmem_limit_bytes=SCOPED),
        cost_estimate=SHORT,
        name="prompt_out",
    )(*[near(value) for value in args], *after)


def pair_product(left, right):
    pairs = left.shape[0]
    left = left.reshape(pairs, DK, 2, DK)
    right = right.reshape(pairs, DK, 2, DV)
    return jnp.einsum("pihj,pjhv->pihv", left, right, precision=HIGH).reshape(pairs, DK, W2)


def send(value, source, target):
    return lax.ppermute(value, "seq", [(source, target)])


class Forward:
    def __init__(self, boths, arrived, skip):
        self.boths, self.size = boths, sum(both.shape[1] for both in boths)
        self.skip = skip
        self.arrived, self.states = [arrived], []

    def advance(self, after):
        hop = len(self.states)
        state = step(hop + 1, self.boths, self.arrived[-1], after, 0 if hop else self.skip)
        self.states.append(state)
        count = lax.axis_size("seq")
        if hop + 2 < count and not (count == 4 and hop == 1):
            self.arrived.append(send(state, hop + 1, hop + 2))
        return (near(state),)


class Backward:
    def __init__(self, both, arrived, direct):
        self.both, self.size, self.direct, self.right = both, both.shape[1], direct, None
        count = lax.axis_size("seq")
        self.half = count // 2
        here = lax.axis_index("seq")
        self.far = arrived
        for source in range(count - 2, self.half, -1):
            sending = jnp.stack(
                [
                    pair_product(arrived[0], both[0]),
                    pair_product(arrived[0], both[1]) + arrived[1],
                ]
            )
            arrived = send(sending, source, source - 1)
            self.far = jnp.where(here == source - 1, arrived, self.far)

    def meet(self, after):
        half = self.half
        state = self.run.states[half - 1]
        self.mid = meet(half, self.far, self.skip, state, after)
        self.lefts = [send(self.mid, half, half - 1)]
        if self.direct:
            self.lefts = [send(self.mid, half, d) for d in range(half - 1)] + self.lefts
        elif half > 2:
            for d in range(half - 2, -1, -1):
                self.lefts.insert(0, send(self.lefts[0], d + 1, d))
        return (near(self.mid),)

    def pass_on(self, after):
        right = (self.run.states[self.half - 1], self.skip)
        left = right if self.direct else (self.lefts[0], 0)
        out = part(self.half, self.size, left, right, after)
        if self.direct:
            self.right = send(out, self.half, self.half + 1)
        else:
            self.right = lax.ppermute(out, "seq", [(1, 0), (2, 3)])
            self.lefts.insert(0, self.right)
        return (near(out),)

    def reach_end(self, after):
        if self.half == 2:
            self.end = step(3, [self.both], self.right, after)
            return (near(self.end),)
        while len(self.run.states) < lax.axis_size("seq") - 1:
            after = self.run.advance(after)
        return after

    def held(self):
        if self.half == 2:
            ends = [(self.end, 0)]
        else:
            ends = [(state, self.skip) for state in self.run.states[self.half :]]
        return [(left, 0) for left in self.lefts] + [(self.mid, 0)] + ends


def settle_runs(backs, after):
    half, count, here = backs[0].half, lax.axis_size("seq"), lax.axis_index("seq")
    final = settle([(back.held(), back.size) for back in backs], after)
    if half > 2:
        inner = (here > half) & (here < count - 1)
        far = jnp.concatenate([back.far for back in backs], axis=1)
        final = jnp.where(inner, pair_product(far[0], final) + far[1], final)
    prompts = lax.axis_size("prompt")
    other = lax.ppermute(final, "prompt", [(i, (i + 1) % prompts) for i in range(prompts)])
    return final, other


def plan_of(pairs):
    if pairs % 8:
        return [[1]] * pairs, [[1]] * pairs, [1] * pairs, [(pairs, pairs)], 0
    u = pairs // 4
    return [[u, u], [u, u // 2, u // 2]], [[2], [2], [1]], [u] * 4, [(2, 2), (3, 2)], 1


FIVE = (
    ("forward", 0),
    ("make", 0),
    ("make", 0),
    ("forward", 1),
    ("forward", 0),
    ("meet", 0),
    ("meet", 1),
    ("pass", 0),
    ("forward", 2),
    ("forward", 1),
    ("meet", 2),
    ("pass", 1),
    ("meet", 3),
    ("end", 0),
    ("forward", 2),
    ("pass", 4),
    ("meet", 4),
    ("pass", 2),
    ("end", 1),
    ("pass", 3),
    ("settle", 0),
    ("make", 0),
    ("land", 4),
    ("end", 2),
    ("end", 3),
    ("end", 4),
    ("settle", 1),
    ("prompt", 0),
    ("out", 0),
    ("out", 1),
)


def order_of(joins, half, makes, groups):
    if half == 2 and joins == [[2], [2], [1]]:
        return FIVE
    forwards, runs = sum(len(join) for join in joins), sum(sum(join) for join in joins)
    order = [("forward", k) for j in range(half) for k in range(forwards)]
    order += [("meet", k) for k in range(runs)]
    order += [("pass", k) for k in range(runs) if half == 2]
    order += [("make", k) for k in range(makes)]
    order += [("end", k) for k in range(runs)]
    order += [("settle", k) for k in range(groups)] + [("prompt", 0)]
    return order + [("out", k) for k in range(groups)]


def local(
    prompt_queries,
    prompt_keys,
    prompt_values,
    prompt_beta,
    prompt_decay,
    suffix_queries,
    suffix_keys,
    suffix_values,
    suffix_beta,
    suffix_decay,
    norm_gain,
    slot_branch,
    branch_length,
    branch_prompt,
):
    gain = norm_gain.reshape(1, DV)
    tables = (slot_branch, branch_length, branch_prompt)
    width = prompt_values.shape[2]
    prompt_in = (prompt_queries, prompt_keys, prompt_values, prompt_beta, prompt_decay)
    suffix_in = (suffix_queries, suffix_keys, suffix_values, suffix_beta, suffix_decay)
    half = lax.axis_size("seq") // 2

    calls, joins, units, groups, direct = plan_of(width // W2)
    total = sum(len(sizes) for sizes in calls)
    boths, terms, packed = [], [], []
    heads_of = [(k, size) for k, join in enumerate(joins) for size in join]
    bounds = [sum(size for k, size in heads_of[:i]) for i in range(len(heads_of) + 1)]

    def pack_up(after):
        while len(packed) < len(boths):
            k = len(packed)
            start = sum(sum(join) for join in joins[:k])
            stop = sum(sum(join) for join in joins[: k + 1])
            if len(boths) < stop:
                break
            packed.append(pack(half, boths[start:stop], boths[k], after))
            after = (near(packed[-1]),)
        return after

    made = []

    def make(after):
        if len(made) == len(units):
            return after
        unit = units[len(made)]
        made.append(suffix_terms(sum(units[: len(made)]), unit, *suffix_in, after=after))
        return (near(made[-1][0]),)

    first, last = 0, ()
    for call, sizes in enumerate(calls):
        new, a, b = prompt_terms(first, sizes, *prompt_in, after=last)
        boths += new
        terms.append((a, b))
        last = pack_up((near(a),))
        if call == 0:
            last = make(last)
        first += sum(sizes)
    opened = [
        lax.ppermute(out, "seq", [(0, 1), (2 * half - 1, 2 * half - 2)]) for out in packed
    ]
    forwards = []
    for i, (k, size) in enumerate(heads_of):
        start = sum(sum(join) for join in joins[:k])
        skip = sum(x.shape[1] for x in boths[start : bounds[i]])
        forwards.append(Forward(boths[bounds[i] : bounds[i + 1]], opened[k], skip))
    backwards = []
    for k, both in enumerate(boths):
        back = Backward(both, opened[k], k + direct >= total)
        f = [i for i in range(len(heads_of)) if bounds[i] <= k][-1]
        back.run = forwards[f]
        back.skip = sum(x.shape[1] for x in boths[bounds[f] : k])
        back.first = sum(x.shape[1] for x in boths[:k])
        backwards.append(back)
    rows = slot_rows(suffix_queries.shape[0], tables, last)
    last = (near(rows),)
    settled = {}
    edges = [sum(runs for runs, count in groups[:i]) for i in range(len(groups) + 1)]
    prompt_out, suffix_out = None, None
    for what, k in order_of(joins, half, len(units), len(groups)):
        if what == "make":
            last = make(last)
        elif what == "forward":
            last = forwards[k].advance(last)
        elif what == "meet":
            last = backwards[k].meet(last)
        elif what == "pass":
            last = backwards[k].pass_on(last)
        elif what == "land":
            last = last + tuple(near(left) for left in backwards[k].lefts)
        elif what == "end":
            last = backwards[k].reach_end(last)
        elif what == "settle":
            settled[k] = settle_runs(backwards[edges[k] : edges[k + 1]], last)
            last = (near(settled[k][0]),)
        elif what == "out":
            done = sum(count for runs, count in groups[:k])
            suffix_out = suffix_outputs(
                backwards[edges[k]].first,
                rows,
                *settled[k],
                made[done : done + groups[k][1]],
                gain,
                suffix_out,
                width,
                last if k == 0 else (),
            )
            last = (away(suffix_out),)
        else:
            lots = [sum(f.size for f, (i, n) in zip(forwards, heads_of) if i == k) for k in range(len(joins))]
            came = [list(zip(opened, lots))]
            for j in range(1, len(forwards[0].arrived)):
                came.append([(f.arrived[j], f.size) for f in forwards])
            if half == 2:
                came.append([(back.right, back.size) for back in backwards])
            prompt_out = prompt_outputs(came, terms, gain, width, last)
            last = (away(prompt_out),)
    return (prompt_out, suffix_out)


def solution(mesh):
    return jax.shard_map(
        local,
        mesh=mesh,
        in_specs=(
            P(("groups", "prompt"), "seq", "head"),
            P(("groups", "prompt"), "seq", "head"),
            P(("groups", "prompt"), "seq", "head"),
            P(("groups", "prompt"), "head", "seq"),
            P(("groups", "prompt"), "head", "seq"),
            P(("groups", "seq", "prompt"), None, "head"),
            P(("groups", "seq", "prompt"), None, "head"),
            P(("groups", "seq", "prompt"), None, "head"),
            P(("groups", "seq", "prompt"), "head", None),
            P(("groups", "seq", "prompt"), "head", None),
            P(),
            P("groups"),
            P("groups"),
            P("groups"),
        ),
        out_specs=(
            P(("groups", "prompt"), "seq", "head"),
            P(("groups", "seq", "prompt"), None, "head"),
        ),
        check_vma=False,
    )
```

```python
import functools
import math

import jax
import jax.numpy as jnp
from jax import lax
from jax.experimental import pallas as pl
from jax.experimental.pallas import tpu as pltpu
from jax.sharding import PartitionSpec as P

DK = 128
DV = 128
CH = 128
W2 = 2 * DV
EPS_NORM = 1e-06
HIGH = lax.Precision.HIGHEST
SCOPED = 24 * 1024 * 1024


def mm(left, right):
    return lax.dot_general(left, right, (((1,), (0,)), ((), ())), preferred_element_type=jnp.float32)


def diag2(pair):
    zero = jnp.zeros((pair.shape[0], DV), pair.dtype)
    top = jnp.concatenate([pair[:, :DV], zero], axis=1)
    low = jnp.concatenate([zero, pair[:, DV:]], axis=1)
    return jnp.concatenate([top, low], axis=0)


def low16(value):
    return value.astype(jnp.bfloat16)


def halves(value):
    high = low16(value)
    return high, low16(value - high.astype(jnp.float32))


def lanes2(col_a, col_b):
    shape = (col_a.shape[0], DV)
    return jnp.concatenate(
        [jnp.broadcast_to(col_a, shape), jnp.broadcast_to(col_b, shape)], axis=1
    )


def unit_rows(vectors):
    wide = vectors.astype(jnp.float32)
    factor = lax.rsqrt(jnp.sum(wide * wide, axis=-1, keepdims=True) + EPS_NORM)
    return low16(wide * factor)


def apply_pair(transfer, state, offset):
    t_hi, t_lo = halves(transfer)
    s_hi, s_lo = halves(state)
    hi = diag2(s_hi)
    return mm(t_hi, hi) + mm(t_lo, hi) + mm(t_hi, diag2(s_lo)) + offset


def gate_tables(decay):
    rows = lax.broadcasted_iota(jnp.int32, (CH, CH), 0)
    cols = lax.broadcasted_iota(jnp.int32, (CH, CH), 1)
    upper = jnp.where(rows <= cols, 1.0, 0.0).astype(jnp.float32)
    cum = lax.dot_general(
        decay, upper, (((1,), (0,)), ((), ())), precision=HIGH, preferred_element_type=jnp.float32
    )
    return cum, cum.T


def chunk_terms(chains):
    rows = lax.broadcasted_iota(jnp.int32, (CH, W2), 0)
    cols = jnp.bitwise_and(lax.broadcasted_iota(jnp.int32, (CH, W2), 1), CH - 1)
    causal = rows >= cols
    eye = jnp.where(rows == cols, 1.0, 0.0).astype(jnp.float32)
    eye16 = low16(eye)
    apart = jnp.bitwise_xor(rows, cols)
    strict = rows > cols
    masks = [
        low16(jnp.where(strict & (apart >= low) & (apart < high), -1.0, 0.0))
        for low, high in ((1, 8), (8, 32), (32, CH))
    ]

    heads = []
    for q, k, v, beta, cum_r, cum_c, ends in chains:
        qn = unit_rows(q)
        kn = unit_rows(k)
        heads.append((qn, kn, low16(kn.astype(jnp.float32).T)))
    grams = []
    for one, two in zip(heads[::2], heads[1::2]):
        rows_of = jnp.concatenate(
            [jnp.concatenate(one[1::-1], axis=0), jnp.concatenate(two[1::-1], axis=0)], axis=1
        )
        both = mm(rows_of, diag2(jnp.concatenate([one[2], two[2]], axis=1)))
        grams += [both[:, :DK], both[:, DK:]]
    if len(heads) % 2:
        qn, kn, kt = heads[-1]
        grams.append(mm(jnp.concatenate([kn, qn], axis=0), kt))
    lows, lefts, grows = [], [], []
    for (q, k, v, beta, cum_r, cum_c, ends), (qn, kn, kt), gram in zip(chains, heads, grams):
        kk = gram[:CH]
        qk = gram[CH:]
        bcast = lanes2(cum_c[:, 0:1], cum_c[:, 1:2])
        row = jnp.concatenate([cum_r[0:1], cum_r[1:2]], axis=1)
        gate = jnp.concatenate([beta[0:1], beta[1:2]], axis=1)
        scaled = jnp.exp(jnp.where(causal, bcast - row, -1e30)) * gate
        lows.append(low16(scaled * jnp.concatenate([kk, kk], axis=1)))
        attn = scaled * jnp.concatenate([qk, qk], axis=1)
        last = jnp.concatenate([cum_r[0:1, CH - 1 :], cum_r[1:2, CH - 1 :]], axis=0)
        last = jnp.concatenate(
            [jnp.broadcast_to(last[0:1], (1, DV)), jnp.broadcast_to(last[1:2], (1, DV))], axis=1
        )
        tail = jnp.exp(last - row) * gate
        ktf = kt.astype(jnp.float32)
        if ends:
            lefts.append(halves(attn))
        else:
            tail_k = jnp.concatenate([ktf, ktf], axis=1) * tail
            lefts.append(halves(jnp.concatenate([attn, tail_k], axis=0)))
        grows.append((jnp.exp(bcast), jnp.exp(row), jnp.exp(last)))
    nil = [low * masks[0] for low in lows]
    sq = [low16(mm(n, diag2(n))) for n in nil]
    fourth = [low16(mm(s, diag2(s))) for s in sq]
    inv = [low16(mm(eye16 + n, diag2(eye16 + s))) for n, s in zip(nil, sq)]
    inv = [low16(mm(i, diag2(eye16 + f))) for i, f in zip(inv, fourth)]
    for mask in masks[1:]:
        x = [low16(mm(i, diag2(low * mask))) for i, low in zip(inv, lows)]
        y = [low16(mm(eye16 + t, diag2(i))) for t, i in zip(x, inv)]
        z = [low16(mm(t, diag2(t))) for t in x]
        full = [mm(eye16 + t, diag2(i)) for t, i in zip(z, y)]
        inv = [low16(f) for f in full]
    ws = [
        low16(mm(low16(f * grow[1]), diag2(jnp.concatenate([kn, kn], axis=1))))
        for f, grow, (qn, kn, kt) in zip(full, grows, heads)
    ]
    us = [halves(mm(i, diag2(chain[2]))) for i, chain in zip(inv, chains)]
    by_w = [mm(left, diag2(w)) for (left, rest), w in zip(lefts, ws)]
    by_u = []
    for (left, rest), (u_hi, u_lo) in zip(lefts, us):
        hi = diag2(u_hi)
        by_u.append(mm(left, hi) + mm(rest, hi) + mm(left, diag2(u_lo)))
    out = []
    for (qn, kn, kt), grow, bw, bu in zip(heads, grows, by_w, by_u):
        qf = qn.astype(jnp.float32)
        a = jnp.concatenate([qf, qf], axis=1) * grow[0] - bw[:CH]
        if bw.shape[0] == CH:
            out.append((a, bu, None, None))
        else:
            out.append((a, bu[:CH], eye * grow[2] - bw[CH:], bu[CH:]))
    return out


def read_chains(pairs, heads, at, q_ref, k_ref, v_ref, beta_ref, decay_ref, slot, skip=0, ends=False):
    beta = beta_ref[slot, heads, at]
    cum_r, cum_c = gate_tables(decay_ref[slot, heads, at])
    return [
        (
            q_ref[slot, at, (skip + p) * DK : (skip + p + 1) * DK],
            k_ref[slot, at, (skip + p) * DK : (skip + p + 1) * DK],
            v_ref[slot, at, (skip + p) * W2 : (skip + p + 1) * W2],
            beta[2 * p : 2 * p + 2],
            cum_r[2 * p : 2 * p + 2],
            cum_c[:, 2 * p : 2 * p + 2],
            ends,
        )
        for p in range(pairs)
    ]


def window(first, pairs):
    return math.gcd(first, pairs) if first else pairs


def lane_specs(arrays, first, pairs, width):
    wide = window(first, pairs)
    specs, args = [], []
    for part in range(first, first + pairs, wide):
        specs.append(
            pl.BlockSpec(arrays.shape[:2] + (wide * width,), lambda i, at=part // wide: (0, 0, at))
        )
        args.append(arrays)
    return specs, args, wide


ANY = pl.BlockSpec(memory_space=pl.ANY)
WHOLE = pl.BlockSpec(memory_space=pltpu.VMEM)


SHORT = pl.CostEstimate(flops=1, transcendentals=0, bytes_accessed=1)


def near(value):
    return pltpu.with_memory_space_constraint(value, pltpu.VMEM)


def away(value):
    return pltpu.with_memory_space_constraint(value, pltpu.HBM)


class Spans:
    def __init__(self, refs, wide, width):
        self.refs, self.size, self.width = refs, wide * width, width

    def __getitem__(self, key):
        lanes = key[-1]
        part, at = divmod(lanes.start, self.size)
        return self.refs[part][key[:-1] + (slice(at, at + lanes.stop - lanes.start),)]


def places_of(sizes):
    return [(run, at) for run, size in enumerate(sizes) for at in range(size)]


def prompt_kernel(first, sizes, wide, count, *refs):
    pairs = sum(sizes)
    q_ref = Spans(refs[:count], wide, DK)
    k_ref = Spans(refs[count : 2 * count], wide, DK)
    v_ref = Spans(refs[2 * count : 3 * count], wide, W2)
    beta_ref, decay_ref = refs[3 * count : 3 * count + 2]
    *both, a_ref, b_ref = refs[len(refs) - 2 - len(sizes) :]
    heads = slice(2 * first, 2 * (first + pairs))
    chains = read_chains(
        pairs, heads, slice(0, CH), q_ref, k_ref, v_ref, beta_ref, decay_ref, 0
    )
    places = places_of(sizes)
    for p, (a, b, transfer, offset) in enumerate(chunk_terms(chains)):
        a_ref[:, p * W2 : (p + 1) * W2] = low16(a)
        b_ref[:, p * W2 : (p + 1) * W2] = low16(b)
        run, at = places[p]
        both[run][0, at] = transfer
        both[run][1, at] = offset


def prompt_terms(first, sizes, q, k, v, beta, decay, after=()):
    pairs = sum(sizes)
    q_specs, q_args, wide = lane_specs(q, first, pairs, DK)
    k_specs, k_args, wide = lane_specs(k, first, pairs, DK)
    v_specs, v_args, wide = lane_specs(v, first, pairs, W2)
    *boths, a, b = pl.pallas_call(
        functools.partial(prompt_kernel, first, sizes, wide, len(q_args)),
        grid=(1,),
        in_specs=q_specs
        + k_specs
        + v_specs
        + [
            pl.BlockSpec(beta.shape, lambda i: (0, 0, 0)),
            pl.BlockSpec(decay.shape, lambda i: (0, 0, 0)),
        ]
        + [ANY] * len(after),
        out_specs=[WHOLE] * (len(sizes) + 2),
        out_shape=[pltpu.VMEM((2, size, DK, W2), jnp.float32) for size in sizes]
        + [pltpu.VMEM((CH, pairs * W2), jnp.bfloat16)] * 2,
        compiler_params=pltpu.CompilerParams(vmem_limit_bytes=SCOPED),
        cost_estimate=SHORT,
        name="prompt_terms",
    )(*[away(value) for value in (*q_args, *k_args, *v_args, beta, decay)], *after)
    return boths, a, b


def suffix_kernel(first, unit, q_ref, k_ref, v_ref, beta_ref, decay_ref, *refs):
    a_ref, b_ref = refs[-2:]
    slots, tokens = q_ref.shape[:2]
    spans = tokens // CH
    heads = slice(2 * first, 2 * (first + unit))
    chains = []
    for slot in range(slots):
        for s in range(spans):
            at = slice(s * CH, (s + 1) * CH)
            chains += read_chains(
                unit, heads, at, q_ref, k_ref, v_ref, beta_ref, decay_ref, slot, first, s + 1 == spans
            )
    terms = chunk_terms(chains)
    for slot in range(slots):
        for p in range(unit):
            lanes = slice(p * W2, (p + 1) * W2)
            a, b, transfer, offset = terms[slot * spans * unit + p]
            a_ref[slot, 0:CH, lanes] = low16(a)
            b_ref[slot, 0:CH, lanes] = low16(b)
            for s in range(1, spans):
                a, b, t_next, o_next = terms[(slot * spans + s) * unit + p]
                a16 = low16(a)
                at = slice(s * CH, (s + 1) * CH)
                d_t = diag2(low16(transfer))
                d_o = diag2(low16(offset))
                a_ref[slot, at, lanes] = low16(mm(a16, d_t))
                b_ref[slot, at, lanes] = low16(mm(a16, d_o) + b)
                if s + 1 < spans:
                    t16 = low16(t_next)
                    transfer, offset = mm(t16, d_t), mm(t16, d_o) + o_next


def suffix_terms(first, unit, q, k, v, beta, decay, after=()):
    slots, tokens = q.shape[0], q.shape[1]
    return pl.pallas_call(
        functools.partial(suffix_kernel, first, unit),
        in_specs=[WHOLE] * 5 + [ANY] * len(after),
        out_specs=[WHOLE] * 2,
        out_shape=[pltpu.VMEM((slots, tokens, unit * W2), jnp.bfloat16)] * 2,
        compiler_params=pltpu.CompilerParams(vmem_limit_bytes=SCOPED),
        cost_estimate=SHORT,
        name="suffix_terms",
    )(near(q), near(k), near(v), near(beta), near(decay), *after)


def call_near(kernel, shapes, name, args, after=(), scratch=()):
    out = pl.pallas_call(
        kernel,
        in_specs=[WHOLE] * len(args) + [ANY] * len(after),
        out_specs=[WHOLE] * len(shapes),
        out_shape=[pltpu.VMEM(shape, jnp.float32) for shape in shapes],
        scratch_shapes=scratch,
        compiler_params=pltpu.CompilerParams(vmem_limit_bytes=SCOPED),
        cost_estimate=SHORT,
        name=name,
    )(*[near(value) for value in args], *after)
    return list(out)


def pair_at(ref, index):
    if len(ref.shape) == 3:
        return ref[index]
    return ref[index // ref.shape[1], index % ref.shape[1]]


def pack_kernel(half, sizes, *refs):
    both_ref, out_ref = refs[len(sizes)], refs[-1]
    here = lax.axis_index("seq")

    @pl.when(here < half)
    def _():
        for p, (run, at) in enumerate(places_of(sizes)):
            out_ref[p // out_ref.shape[1], p % out_ref.shape[1]] = refs[run][1, at]

    @pl.when(here >= half)
    def _():
        out_ref[...] = both_ref[...]


def pack(half, boths, both, after):
    sizes = [other.shape[1] for other in boths]
    (out,) = call_near(
        functools.partial(pack_kernel, half, sizes), [both.shape], "pack", [*boths, both], after
    )
    return out


def part_kernel(half, skips, left_ref, state_ref, *refs):
    out_ref = refs[-1]
    here = lax.axis_index("seq")

    @pl.when(here < half)
    def _():
        out_ref[...] = left_ref[skips[0] : skips[0] + out_ref.shape[0]]

    @pl.when(here >= half)
    def _():
        out_ref[...] = state_ref[skips[1] : skips[1] + out_ref.shape[0]]


def part(half, size, left, right, after):
    (out,) = call_near(
        functools.partial(part_kernel, half, (left[1], right[1])),
        [(size, DK, W2)],
        "part",
        [left[0], right[0]],
        after,
    )
    return out


def step_kernel(user, sizes, skip, *refs):
    state_ref, out_ref = refs[len(sizes)], refs[-1]

    @pl.when(lax.axis_index("seq") == user)
    def _():
        for p, (run, at) in enumerate(places_of(sizes)):
            out_ref[p] = apply_pair(refs[run][0, at], pair_at(state_ref, skip + p), refs[run][1, at])


def step(user, boths, state, after, skip=0):
    sizes = [both.shape[1] for both in boths]
    (out,) = call_near(
        functools.partial(step_kernel, user, sizes, skip),
        [(sum(sizes), DK, W2)],
        "state_step",
        [*boths, state],
        after,
    )
    return out


def meet_kernel(user, skip, far_ref, state_ref, *refs):
    out_ref = refs[-1]

    @pl.when(lax.axis_index("seq") == user)
    def _():
        for p in range(out_ref.shape[0]):
            out_ref[p] = apply_pair(far_ref[0, p], state_ref[skip + p], far_ref[1, p])


def meet(user, far, skip, state, after):
    (out,) = call_near(
        functools.partial(meet_kernel, user, skip),
        [far.shape[1:]],
        "final_state",
        [far, state],
        after,
    )
    return out


def settle_kernel(sizes, skips, *refs):
    here = lax.axis_index("seq")
    out_ref = refs[-1]
    wide = len(skips[0])
    at = 0
    for run, size in enumerate(sizes):
        for d, skip in enumerate(skips[run]):

            @pl.when(here == d)
            def _(at=at, size=size, skip=skip, source=refs[run * wide + d]):
                out_ref[at : at + size] = source[skip : skip + size]

        at += size


def settle(runs, after):
    sizes = [size for held, size in runs]
    (out,) = call_near(
        functools.partial(settle_kernel, sizes, [[skip for x, skip in held] for held, size in runs]),
        [(sum(sizes), DK, W2)],
        "settle",
        [x for held, size in runs for x, skip in held],
        after,
    )
    return out


def slot_rows_kernel(slots, n_prompt, sb_ref, bl_ref, bp_ref, *refs):
    out_ref = refs[-1]
    me = lax.axis_index("prompt")
    rank = lax.axis_index("seq") * n_prompt + me
    for slot in range(slots):
        branch = sb_ref[rank * slots + slot]
        mine = jnp.where(bp_ref[branch] == me, 1, 0)
        out_ref[slot, 0:8] = jnp.full((8, W2), bl_ref[branch], jnp.int32)
        out_ref[slot, 8:16] = jnp.full((8, W2), mine, jnp.int32)


def slot_rows(slots, tables, after):
    return pl.pallas_call(
        functools.partial(slot_rows_kernel, slots, lax.axis_size("prompt")),
        in_specs=[pl.BlockSpec(memory_space=pltpu.SMEM)] * 3 + [ANY] * len(after),
        out_specs=WHOLE,
        out_shape=pltpu.VMEM((slots, 16, W2), jnp.int32),
        compiler_params=pltpu.CompilerParams(vmem_limit_bytes=SCOPED),
        cost_estimate=SHORT,
        name="slot_rows",
    )(*tables, *after)


def finish(a, state, b, gain2):
    raw = mm(a, diag2(low16(state))) + b.astype(jnp.float32)
    share = diag2(jnp.full((DV, W2), 1.0 / DV, jnp.bfloat16))
    return raw * lax.rsqrt(mm(low16(raw * raw), share) + EPS_NORM) * gain2


def suffix_out_kernel(sizes, *refs):
    rows_ref, own_ref, other_ref, gain_ref = refs[:4]
    out_ref = refs[-1]
    slot = pl.program_id(0)
    mine = rows_ref[slot, 8:9] == 1
    gain = gain_ref[...]
    gain2 = jnp.concatenate([gain, gain], axis=1)
    tokens = out_ref.shape[1]
    live = lax.broadcasted_iota(jnp.int32, (tokens, W2), 0) < rows_ref[slot, 0:1]
    for p, (run, at) in enumerate(places_of(sizes)):
        source = slice(at * W2, (at + 1) * W2)
        a_ref, b_ref = refs[4 + 2 * run : 6 + 2 * run]
        state = jnp.where(mine, own_ref[p], other_ref[p])
        out = finish(a_ref[slot, :, source], state, b_ref[slot, :, source], gain2)
        out_ref[0, :, p * W2 : (p + 1) * W2] = low16(jnp.where(live, out, 0.0))


def suffix_outputs(first, rows, own, other, terms, gain, so_far, width, after=()):
    slots, tokens, _ = terms[0][0].shape
    sizes = [a.shape[2] // W2 for a, b in terms]
    pairs = sum(sizes)
    at = first // pairs
    args = [rows, own, other, gain] + [x for pair in terms for x in pair]
    in_specs = [WHOLE] * len(args)
    args = [near(value) for value in args]
    aliases = {}
    if so_far is not None:
        aliases = {len(args): 0}
        in_specs.append(ANY)
        args.append(away(so_far))
    return pl.pallas_call(
        functools.partial(suffix_out_kernel, sizes),
        grid=(slots,),
        in_specs=in_specs + [ANY] * len(after),
        out_specs=pl.BlockSpec((1, tokens, pairs * W2), lambda i: (i, 0, at)),
        out_shape=pltpu.HBM((slots, tokens, width), jnp.bfloat16),
        input_output_aliases=aliases,
        compiler_params=pltpu.CompilerParams(vmem_limit_bytes=SCOPED),
        cost_estimate=SHORT,
        name="suffix_out",
    )(*args, *after)


def prompt_out_kernel(calls, hops, *refs):
    here = lax.axis_index("seq")
    refs, out_ref, state_ref = list(refs[:-2]), refs[-2], refs[-1]
    for j, sizes in enumerate(hops):
        arrived = [refs.pop(0) for _ in sizes]

        @pl.when((here == j + 1) | ((here == 0) & (j == 0)))
        def _(sizes=sizes, arrived=arrived):
            for p, (run, at) in enumerate(places_of(sizes)):
                state_ref[p] = pair_at(arrived[run], at)

    terms = [(refs.pop(0), refs.pop(0)) for _ in calls]
    gain = refs[0][...]
    gain2 = jnp.concatenate([gain, gain], axis=1)
    for p, (call, at) in enumerate(places_of(calls)):
        source = slice(at * W2, (at + 1) * W2)
        a_ref, b_ref = terms[call]
        out = finish(a_ref[:, source], state_ref[p], b_ref[:, source], gain2)
        out_ref[0, :, p * W2 : (p + 1) * W2] = low16(out)


def prompt_outputs(arrived, terms, gain, width, after=()):
    pairs = width // W2
    calls = [a.shape[1] // W2 for a, b in terms]
    hops = [[size for x, size in hop] for hop in arrived]
    args = [x for hop in arrived for x, size in hop] + [x for pair in terms for x in pair] + [gain]
    return pl.pallas_call(
        functools.partial(prompt_out_kernel, calls, hops),
        grid=(1,),
        in_specs=[WHOLE] * len(args) + [ANY] * len(after),
        out_specs=pl.BlockSpec((1, CH, width), lambda i: (0, 0, 0)),
        out_shape=pltpu.HBM((1, CH, width), jnp.bfloat16),
        scratch_shapes=[pltpu.VMEM((pairs, DK, W2), jnp.float32)],
        compiler_params=pltpu.CompilerParams(vmem_limit_bytes=SCOPED),
        cost_estimate=SHORT,
        name="prompt_out",
    )(*[near(value) for value in args], *after)


def pair_product(left, right):
    pairs = left.shape[0]
    left = left.reshape(pairs, DK, 2, DK)
    right = right.reshape(pairs, DK, 2, DV)
    return jnp.einsum("pihj,pjhv->pihv", left, right, precision=HIGH).reshape(pairs, DK, W2)


def send(value, source, target):
    return lax.ppermute(value, "seq", [(source, target)])


class Forward:
    def __init__(self, boths, arrived, skip):
        self.boths, self.size = boths, sum(both.shape[1] for both in boths)
        self.skip = skip
        self.arrived, self.states = [arrived], []

    def advance(self, after):
        hop = len(self.states)
        state = step(hop + 1, self.boths, self.arrived[-1], after, 0 if hop else self.skip)
        self.states.append(state)
        count = lax.axis_size("seq")
        if hop + 2 < count and not (count == 4 and hop == 1):
            self.arrived.append(send(state, hop + 1, hop + 2))
        return (near(state),)


class Backward:
    def __init__(self, both, arrived, direct):
        self.both, self.size, self.direct, self.right = both, both.shape[1], direct, None
        count = lax.axis_size("seq")
        self.half = count // 2
        here = lax.axis_index("seq")
        self.far = arrived
        for source in range(count - 2, self.half, -1):
            sending = jnp.stack(
                [
                    pair_product(arrived[0], both[0]),
                    pair_product(arrived[0], both[1]) + arrived[1],
                ]
            )
            arrived = send(sending, source, source - 1)
            self.far = jnp.where(here == source - 1, arrived, self.far)

    def meet(self, after):
        half = self.half
        state = self.run.states[half - 1]
        self.mid = meet(half, self.far, self.skip, state, after)
        self.lefts = [send(self.mid, half, half - 1)]
        if self.direct:
            self.lefts = [send(self.mid, half, d) for d in range(half - 1)] + self.lefts
        elif half > 2:
            for d in range(half - 2, -1, -1):
                self.lefts.insert(0, send(self.lefts[0], d + 1, d))
        return (near(self.mid),)

    def pass_on(self, after):
        right = (self.run.states[self.half - 1], self.skip)
        left = right if self.direct else (self.lefts[0], 0)
        out = part(self.half, self.size, left, right, after)
        if self.direct:
            self.right = send(out, self.half, self.half + 1)
        else:
            self.right = lax.ppermute(out, "seq", [(1, 0), (2, 3)])
            self.lefts.insert(0, self.right)
        return (near(out),)

    def reach_end(self, after):
        if self.half == 2:
            self.end = step(3, [self.both], self.right, after)
            return (near(self.end),)
        while len(self.run.states) < lax.axis_size("seq") - 1:
            after = self.run.advance(after)
        return after

    def held(self):
        if self.half == 2:
            ends = [(self.end, 0)]
        else:
            ends = [(state, self.skip) for state in self.run.states[self.half :]]
        return [(left, 0) for left in self.lefts] + [(self.mid, 0)] + ends


def settle_runs(backs, after):
    half, count, here = backs[0].half, lax.axis_size("seq"), lax.axis_index("seq")
    final = settle([(back.held(), back.size) for back in backs], after)
    if half > 2:
        inner = (here > half) & (here < count - 1)
        far = jnp.concatenate([back.far for back in backs], axis=1)
        final = jnp.where(inner, pair_product(far[0], final) + far[1], final)
    prompts = lax.axis_size("prompt")
    other = lax.ppermute(final, "prompt", [(i, (i + 1) % prompts) for i in range(prompts)])
    return final, other


def plan_of(pairs):
    if pairs % 8:
        return [[1]] * pairs, [[1]] * pairs, [1] * pairs, [(pairs, pairs)], 0
    u = pairs // 4
    return [[u, u], [u, u // 2, u // 2]], [[2], [2], [1]], [u] * 4, [(2, 2), (3, 2)], 1


FIVE = (
    ("forward", 0),
    ("make", 0),
    ("make", 0),
    ("forward", 1),
    ("forward", 0),
    ("meet", 0),
    ("meet", 1),
    ("pass", 0),
    ("forward", 2),
    ("forward", 1),
    ("meet", 2),
    ("pass", 1),
    ("meet", 3),
    ("end", 0),
    ("forward", 2),
    ("pass", 4),
    ("meet", 4),
    ("pass", 2),
    ("pass", 3),
    ("make", 0),
    ("end", 1),
    ("settle", 0),
    ("land", 4),
    ("end", 2),
    ("end", 3),
    ("end", 4),
    ("settle", 1),
    ("prompt", 0),
    ("out", 0),
    ("out", 1),
)


def order_of(joins, half, makes, groups):
    if half == 2 and joins == [[2], [2], [1]]:
        return FIVE
    forwards, runs = sum(len(join) for join in joins), sum(sum(join) for join in joins)
    order = [("forward", k) for j in range(half) for k in range(forwards)]
    order += [("meet", k) for k in range(runs)]
    order += [("pass", k) for k in range(runs) if half == 2]
    order += [("make", k) for k in range(makes)]
    order += [("end", k) for k in range(runs)]
    order += [("settle", k) for k in range(groups)] + [("prompt", 0)]
    return order + [("out", k) for k in range(groups)]


def local(
    prompt_queries,
    prompt_keys,
    prompt_values,
    prompt_beta,
    prompt_decay,
    suffix_queries,
    suffix_keys,
    suffix_values,
    suffix_beta,
    suffix_decay,
    norm_gain,
    slot_branch,
    branch_length,
    branch_prompt,
):
    gain = norm_gain.reshape(1, DV)
    tables = (slot_branch, branch_length, branch_prompt)
    width = prompt_values.shape[2]
    prompt_in = (prompt_queries, prompt_keys, prompt_values, prompt_beta, prompt_decay)
    suffix_in = (suffix_queries, suffix_keys, suffix_values, suffix_beta, suffix_decay)
    half = lax.axis_size("seq") // 2

    calls, joins, units, groups, direct = plan_of(width // W2)
    total = sum(len(sizes) for sizes in calls)
    boths, terms, packed = [], [], []
    heads_of = [(k, size) for k, join in enumerate(joins) for size in join]
    bounds = [sum(size for k, size in heads_of[:i]) for i in range(len(heads_of) + 1)]

    def pack_up(after):
        while len(packed) < len(boths):
            k = len(packed)
            start = sum(sum(join) for join in joins[:k])
            stop = sum(sum(join) for join in joins[: k + 1])
            if len(boths) < stop:
                break
            packed.append(pack(half, boths[start:stop], boths[k], after))
            after = (near(packed[-1]),)
        return after

    made = []

    def make(after):
        if len(made) == len(units):
            return after
        unit = units[len(made)]
        made.append(suffix_terms(sum(units[: len(made)]), unit, *suffix_in, after=after))
        return (near(made[-1][0]),)

    first, last = 0, ()
    for call, sizes in enumerate(calls):
        new, a, b = prompt_terms(first, sizes, *prompt_in, after=last)
        boths += new
        terms.append((a, b))
        last = pack_up((near(a),))
        if call == 0:
            last = make(last)
        first += sum(sizes)
    opened = [
        lax.ppermute(out, "seq", [(0, 1), (2 * half - 1, 2 * half - 2)]) for out in packed
    ]
    forwards = []
    for i, (k, size) in enumerate(heads_of):
        start = sum(sum(join) for join in joins[:k])
        skip = sum(x.shape[1] for x in boths[start : bounds[i]])
        forwards.append(Forward(boths[bounds[i] : bounds[i + 1]], opened[k], skip))
    backwards = []
    for k, both in enumerate(boths):
        back = Backward(both, opened[k], k + direct >= total)
        f = [i for i in range(len(heads_of)) if bounds[i] <= k][-1]
        back.run = forwards[f]
        back.skip = sum(x.shape[1] for x in boths[bounds[f] : k])
        back.first = sum(x.shape[1] for x in boths[:k])
        backwards.append(back)
    rows = slot_rows(suffix_queries.shape[0], tables, last)
    last = (near(rows),)
    settled = {}
    edges = [sum(runs for runs, count in groups[:i]) for i in range(len(groups) + 1)]
    prompt_out, suffix_out = None, None
    for what, k in order_of(joins, half, len(units), len(groups)):
        if what == "make":
            last = make(last)
        elif what == "forward":
            last = forwards[k].advance(last)
        elif what == "meet":
            last = backwards[k].meet(last)
        elif what == "pass":
            last = backwards[k].pass_on(last)
        elif what == "land":
            last = last + tuple(near(left) for left in backwards[k].lefts)
        elif what == "end":
            last = backwards[k].reach_end(last)
        elif what == "settle":
            settled[k] = settle_runs(backwards[edges[k] : edges[k + 1]], last)
            last = (near(settled[k][0]),)
        elif what == "out":
            done = sum(count for runs, count in groups[:k])
            suffix_out = suffix_outputs(
                backwards[edges[k]].first,
                rows,
                *settled[k],
                made[done : done + groups[k][1]],
                gain,
                suffix_out,
                width,
                last if k == 0 else (),
            )
            last = (away(suffix_out),)
        else:
            lots = [sum(f.size for f, (i, n) in zip(forwards, heads_of) if i == k) for k in range(len(joins))]
            came = [list(zip(opened, lots))]
            for j in range(1, len(forwards[0].arrived)):
                came.append([(f.arrived[j], f.size) for f in forwards])
            if half == 2:
                came.append([(back.right, back.size) for back in backwards])
            prompt_out = prompt_outputs(came, terms, gain, width, last)
            last = (away(prompt_out),)
    return (prompt_out, suffix_out)


def solution(mesh):
    return jax.shard_map(
        local,
        mesh=mesh,
        in_specs=(
            P(("groups", "prompt"), "seq", "head"),
            P(("groups", "prompt"), "seq", "head"),
            P(("groups", "prompt"), "seq", "head"),
            P(("groups", "prompt"), "head", "seq"),
            P(("groups", "prompt"), "head", "seq"),
            P(("groups", "seq", "prompt"), None, "head"),
            P(("groups", "seq", "prompt"), None, "head"),
            P(("groups", "seq", "prompt"), None, "head"),
            P(("groups", "seq", "prompt"), "head", None),
            P(("groups", "seq", "prompt"), "head", None),
            P(),
            P("groups"),
            P("groups"),
            P("groups"),
        ),
        out_specs=(
            P(("groups", "prompt"), "seq", "head"),
            P(("groups", "seq", "prompt"), None, "head"),
        ),
        check_vma=False,
    )
```

```python
import functools
import math

import jax
import jax.numpy as jnp
from jax import lax
from jax.experimental import pallas as pl
from jax.experimental.pallas import tpu as pltpu
from jax.sharding import PartitionSpec as P

DK = 128
DV = 128
CH = 128
W2 = 2 * DV
EPS_NORM = 1e-06
HIGH = lax.Precision.HIGHEST
SCOPED = 24 * 1024 * 1024


def mm(left, right):
    return lax.dot_general(left, right, (((1,), (0,)), ((), ())), preferred_element_type=jnp.float32)


def diag2(pair):
    zero = jnp.zeros((pair.shape[0], DV), pair.dtype)
    top = jnp.concatenate([pair[:, :DV], zero], axis=1)
    low = jnp.concatenate([zero, pair[:, DV:]], axis=1)
    return jnp.concatenate([top, low], axis=0)


def low16(value):
    return value.astype(jnp.bfloat16)


def halves(value):
    high = low16(value)
    return high, low16(value - high.astype(jnp.float32))


def lanes2(col_a, col_b):
    shape = (col_a.shape[0], DV)
    return jnp.concatenate(
        [jnp.broadcast_to(col_a, shape), jnp.broadcast_to(col_b, shape)], axis=1
    )


def unit_rows(vectors):
    wide = vectors.astype(jnp.float32)
    factor = lax.rsqrt(jnp.sum(wide * wide, axis=-1, keepdims=True) + EPS_NORM)
    return low16(wide * factor)


def apply_pair(transfer, state, offset):
    t_hi, t_lo = halves(transfer)
    s_hi, s_lo = halves(state)
    hi = diag2(s_hi)
    return mm(t_hi, hi) + mm(t_lo, hi) + mm(t_hi, diag2(s_lo)) + offset


def gate_tables(decay):
    rows = lax.broadcasted_iota(jnp.int32, (CH, CH), 0)
    cols = lax.broadcasted_iota(jnp.int32, (CH, CH), 1)
    upper = jnp.where(rows <= cols, 1.0, 0.0).astype(jnp.float32)
    cum = lax.dot_general(
        decay, upper, (((1,), (0,)), ((), ())), precision=HIGH, preferred_element_type=jnp.float32
    )
    return cum, cum.T


def chunk_terms(chains):
    rows = lax.broadcasted_iota(jnp.int32, (CH, W2), 0)
    cols = jnp.bitwise_and(lax.broadcasted_iota(jnp.int32, (CH, W2), 1), CH - 1)
    causal = rows >= cols
    eye = jnp.where(rows == cols, 1.0, 0.0).astype(jnp.float32)
    eye16 = low16(eye)
    apart = jnp.bitwise_xor(rows, cols)
    strict = rows > cols
    masks = [
        low16(jnp.where(strict & (apart >= low) & (apart < high), -1.0, 0.0))
        for low, high in ((1, 8), (8, 32), (32, CH))
    ]

    heads = []
    for q, k, v, beta, cum_r, cum_c, ends in chains:
        qn = unit_rows(q)
        kn = unit_rows(k)
        heads.append((qn, kn, low16(kn.astype(jnp.float32).T)))
    grams = []
    for one, two in zip(heads[::2], heads[1::2]):
        rows_of = jnp.concatenate(
            [jnp.concatenate(one[1::-1], axis=0), jnp.concatenate(two[1::-1], axis=0)], axis=1
        )
        both = mm(rows_of, diag2(jnp.concatenate([one[2], two[2]], axis=1)))
        grams += [both[:, :DK], both[:, DK:]]
    if len(heads) % 2:
        qn, kn, kt = heads[-1]
        grams.append(mm(jnp.concatenate([kn, qn], axis=0), kt))
    lows, lefts, grows = [], [], []
    for (q, k, v, beta, cum_r, cum_c, ends), (qn, kn, kt), gram in zip(chains, heads, grams):
        kk = gram[:CH]
        qk = gram[CH:]
        bcast = lanes2(cum_c[:, 0:1], cum_c[:, 1:2])
        row = jnp.concatenate([cum_r[0:1], cum_r[1:2]], axis=1)
        gate = jnp.concatenate([beta[0:1], beta[1:2]], axis=1)
        scaled = jnp.exp(jnp.where(causal, bcast - row, -1e30)) * gate
        lows.append(low16(scaled * jnp.concatenate([kk, kk], axis=1)))
        attn = scaled * jnp.concatenate([qk, qk], axis=1)
        last = jnp.concatenate([cum_r[0:1, CH - 1 :], cum_r[1:2, CH - 1 :]], axis=0)
        last = jnp.concatenate(
            [jnp.broadcast_to(last[0:1], (1, DV)), jnp.broadcast_to(last[1:2], (1, DV))], axis=1
        )
        tail = jnp.exp(last - row) * gate
        ktf = kt.astype(jnp.float32)
        if ends:
            lefts.append(halves(attn))
        else:
            tail_k = jnp.concatenate([ktf, ktf], axis=1) * tail
            lefts.append(halves(jnp.concatenate([attn, tail_k], axis=0)))
        grows.append((jnp.exp(bcast), jnp.exp(row), jnp.exp(last)))
    nil = [low * masks[0] for low in lows]
    sq = [low16(mm(n, diag2(n))) for n in nil]
    fourth = [low16(mm(s, diag2(s))) for s in sq]
    inv = [low16(mm(eye16 + n, diag2(eye16 + s))) for n, s in zip(nil, sq)]
    inv = [low16(mm(i, diag2(eye16 + f))) for i, f in zip(inv, fourth)]
    for mask in masks[1:]:
        x = [low16(mm(i, diag2(low * mask))) for i, low in zip(inv, lows)]
        y = [low16(mm(eye16 + t, diag2(i))) for t, i in zip(x, inv)]
        z = [low16(mm(t, diag2(t))) for t in x]
        full = [mm(eye16 + t, diag2(i)) for t, i in zip(z, y)]
        inv = [low16(f) for f in full]
    ws = [
        low16(mm(low16(f * grow[1]), diag2(jnp.concatenate([kn, kn], axis=1))))
        for f, grow, (qn, kn, kt) in zip(full, grows, heads)
    ]
    us = [halves(mm(i, diag2(chain[2]))) for i, chain in zip(inv, chains)]
    by_w = [mm(left, diag2(w)) for (left, rest), w in zip(lefts, ws)]
    by_u = []
    for (left, rest), (u_hi, u_lo) in zip(lefts, us):
        hi = diag2(u_hi)
        by_u.append(mm(left, hi) + mm(rest, hi) + mm(left, diag2(u_lo)))
    out = []
    for (qn, kn, kt), grow, bw, bu in zip(heads, grows, by_w, by_u):
        qf = qn.astype(jnp.float32)
        a = jnp.concatenate([qf, qf], axis=1) * grow[0] - bw[:CH]
        if bw.shape[0] == CH:
            out.append((a, bu, None, None))
        else:
            out.append((a, bu[:CH], eye * grow[2] - bw[CH:], bu[CH:]))
    return out


def read_chains(pairs, heads, at, q_ref, k_ref, v_ref, beta_ref, decay_ref, slot, skip=0, ends=False):
    beta = beta_ref[slot, heads, at]
    cum_r, cum_c = gate_tables(decay_ref[slot, heads, at])
    return [
        (
            q_ref[slot, at, (skip + p) * DK : (skip + p + 1) * DK],
            k_ref[slot, at, (skip + p) * DK : (skip + p + 1) * DK],
            v_ref[slot, at, (skip + p) * W2 : (skip + p + 1) * W2],
            beta[2 * p : 2 * p + 2],
            cum_r[2 * p : 2 * p + 2],
            cum_c[:, 2 * p : 2 * p + 2],
            ends,
        )
        for p in range(pairs)
    ]


def window(first, pairs):
    return math.gcd(first, pairs) if first else pairs


def lane_specs(arrays, first, pairs, width):
    wide = window(first, pairs)
    specs, args = [], []
    for part in range(first, first + pairs, wide):
        specs.append(
            pl.BlockSpec(arrays.shape[:2] + (wide * width,), lambda i, at=part // wide: (0, 0, at))
        )
        args.append(arrays)
    return specs, args, wide


ANY = pl.BlockSpec(memory_space=pl.ANY)
WHOLE = pl.BlockSpec(memory_space=pltpu.VMEM)


SHORT = pl.CostEstimate(flops=1, transcendentals=0, bytes_accessed=1)


def near(value):
    return pltpu.with_memory_space_constraint(value, pltpu.VMEM)


def away(value):
    return pltpu.with_memory_space_constraint(value, pltpu.HBM)


class Spans:
    def __init__(self, refs, wide, width):
        self.refs, self.size, self.width = refs, wide * width, width

    def __getitem__(self, key):
        lanes = key[-1]
        part, at = divmod(lanes.start, self.size)
        return self.refs[part][key[:-1] + (slice(at, at + lanes.stop - lanes.start),)]


def places_of(sizes):
    return [(run, at) for run, size in enumerate(sizes) for at in range(size)]


def prompt_kernel(first, sizes, wide, count, *refs):
    pairs = sum(sizes)
    q_ref = Spans(refs[:count], wide, DK)
    k_ref = Spans(refs[count : 2 * count], wide, DK)
    v_ref = Spans(refs[2 * count : 3 * count], wide, W2)
    beta_ref, decay_ref = refs[3 * count : 3 * count + 2]
    *both, a_ref, b_ref = refs[len(refs) - 2 - len(sizes) :]
    heads = slice(2 * first, 2 * (first + pairs))
    chains = read_chains(
        pairs, heads, slice(0, CH), q_ref, k_ref, v_ref, beta_ref, decay_ref, 0
    )
    places = places_of(sizes)
    for p, (a, b, transfer, offset) in enumerate(chunk_terms(chains)):
        a_ref[:, p * W2 : (p + 1) * W2] = low16(a)
        b_ref[:, p * W2 : (p + 1) * W2] = low16(b)
        run, at = places[p]
        both[run][0, at] = transfer
        both[run][1, at] = offset


def prompt_terms(first, sizes, q, k, v, beta, decay, after=()):
    pairs = sum(sizes)
    q_specs, q_args, wide = lane_specs(q, first, pairs, DK)
    k_specs, k_args, wide = lane_specs(k, first, pairs, DK)
    v_specs, v_args, wide = lane_specs(v, first, pairs, W2)
    *boths, a, b = pl.pallas_call(
        functools.partial(prompt_kernel, first, sizes, wide, len(q_args)),
        grid=(1,),
        in_specs=q_specs
        + k_specs
        + v_specs
        + [
            pl.BlockSpec(beta.shape, lambda i: (0, 0, 0)),
            pl.BlockSpec(decay.shape, lambda i: (0, 0, 0)),
        ]
        + [ANY] * len(after),
        out_specs=[WHOLE] * (len(sizes) + 2),
        out_shape=[pltpu.VMEM((2, size, DK, W2), jnp.float32) for size in sizes]
        + [pltpu.VMEM((CH, pairs * W2), jnp.bfloat16)] * 2,
        compiler_params=pltpu.CompilerParams(vmem_limit_bytes=SCOPED),
        cost_estimate=SHORT,
        name="prompt_terms",
    )(*[away(value) for value in (*q_args, *k_args, *v_args, beta, decay)], *after)
    return boths, a, b


def suffix_kernel(first, unit, q_ref, k_ref, v_ref, beta_ref, decay_ref, *refs):
    a_ref, b_ref = refs[-2:]
    slots, tokens = q_ref.shape[:2]
    spans = tokens // CH
    heads = slice(2 * first, 2 * (first + unit))
    chains = []
    for slot in range(slots):
        for s in range(spans):
            at = slice(s * CH, (s + 1) * CH)
            chains += read_chains(
                unit, heads, at, q_ref, k_ref, v_ref, beta_ref, decay_ref, slot, first, s + 1 == spans
            )
    terms = chunk_terms(chains)
    for slot in range(slots):
        for p in range(unit):
            lanes = slice(p * W2, (p + 1) * W2)
            a, b, transfer, offset = terms[slot * spans * unit + p]
            a_ref[slot, 0:CH, lanes] = low16(a)
            b_ref[slot, 0:CH, lanes] = low16(b)
            for s in range(1, spans):
                a, b, t_next, o_next = terms[(slot * spans + s) * unit + p]
                a16 = low16(a)
                at = slice(s * CH, (s + 1) * CH)
                d_t = diag2(low16(transfer))
                d_o = diag2(low16(offset))
                a_ref[slot, at, lanes] = low16(mm(a16, d_t))
                b_ref[slot, at, lanes] = low16(mm(a16, d_o) + b)
                if s + 1 < spans:
                    t16 = low16(t_next)
                    transfer, offset = mm(t16, d_t), mm(t16, d_o) + o_next


def suffix_terms(first, unit, q, k, v, beta, decay, after=()):
    slots, tokens = q.shape[0], q.shape[1]
    return pl.pallas_call(
        functools.partial(suffix_kernel, first, unit),
        in_specs=[WHOLE] * 5 + [ANY] * len(after),
        out_specs=[WHOLE] * 2,
        out_shape=[pltpu.VMEM((slots, tokens, unit * W2), jnp.bfloat16)] * 2,
        compiler_params=pltpu.CompilerParams(vmem_limit_bytes=SCOPED),
        cost_estimate=SHORT,
        name="suffix_terms",
    )(near(q), near(k), near(v), near(beta), near(decay), *after)


def call_near(kernel, shapes, name, args, after=(), scratch=()):
    out = pl.pallas_call(
        kernel,
        in_specs=[WHOLE] * len(args) + [ANY] * len(after),
        out_specs=[WHOLE] * len(shapes),
        out_shape=[pltpu.VMEM(shape, jnp.float32) for shape in shapes],
        scratch_shapes=scratch,
        compiler_params=pltpu.CompilerParams(vmem_limit_bytes=SCOPED),
        cost_estimate=SHORT,
        name=name,
    )(*[near(value) for value in args], *after)
    return list(out)


def pair_at(ref, index):
    if len(ref.shape) == 3:
        return ref[index]
    return ref[index // ref.shape[1], index % ref.shape[1]]


def pack_kernel(half, sizes, *refs):
    both_ref, out_ref = refs[len(sizes)], refs[-1]
    here = lax.axis_index("seq")

    @pl.when(here < half)
    def _():
        for p, (run, at) in enumerate(places_of(sizes)):
            out_ref[p // out_ref.shape[1], p % out_ref.shape[1]] = refs[run][1, at]

    @pl.when(here >= half)
    def _():
        out_ref[...] = both_ref[...]


def pack(half, boths, both, after):
    sizes = [other.shape[1] for other in boths]
    (out,) = call_near(
        functools.partial(pack_kernel, half, sizes), [both.shape], "pack", [*boths, both], after
    )
    return out


def part_kernel(half, skips, left_ref, state_ref, *refs):
    out_ref = refs[-1]
    here = lax.axis_index("seq")

    @pl.when(here < half)
    def _():
        out_ref[...] = left_ref[skips[0] : skips[0] + out_ref.shape[0]]

    @pl.when(here >= half)
    def _():
        out_ref[...] = state_ref[skips[1] : skips[1] + out_ref.shape[0]]


def part(half, size, left, right, after):
    (out,) = call_near(
        functools.partial(part_kernel, half, (left[1], right[1])),
        [(size, DK, W2)],
        "part",
        [left[0], right[0]],
        after,
    )
    return out


def step_kernel(user, sizes, skip, *refs):
    state_ref, out_ref = refs[len(sizes)], refs[-1]

    @pl.when(lax.axis_index("seq") == user)
    def _():
        for p, (run, at) in enumerate(places_of(sizes)):
            out_ref[p] = apply_pair(refs[run][0, at], pair_at(state_ref, skip + p), refs[run][1, at])


def step(user, boths, state, after, skip=0):
    sizes = [both.shape[1] for both in boths]
    (out,) = call_near(
        functools.partial(step_kernel, user, sizes, skip),
        [(sum(sizes), DK, W2)],
        "state_step",
        [*boths, state],
        after,
    )
    return out


def meet_kernel(user, skip, far_ref, state_ref, *refs):
    out_ref = refs[-1]

    @pl.when(lax.axis_index("seq") == user)
    def _():
        for p in range(out_ref.shape[0]):
            out_ref[p] = apply_pair(far_ref[0, p], state_ref[skip + p], far_ref[1, p])


def meet(user, far, skip, state, after):
    (out,) = call_near(
        functools.partial(meet_kernel, user, skip),
        [far.shape[1:]],
        "final_state",
        [far, state],
        after,
    )
    return out


def settle_kernel(sizes, skips, *refs):
    here = lax.axis_index("seq")
    out_ref = refs[-1]
    wide = len(skips[0])
    at = 0
    for run, size in enumerate(sizes):
        for d, skip in enumerate(skips[run]):

            @pl.when(here == d)
            def _(at=at, size=size, skip=skip, source=refs[run * wide + d]):
                out_ref[at : at + size] = source[skip : skip + size]

        at += size


def settle(runs, after):
    sizes = [size for held, size in runs]
    (out,) = call_near(
        functools.partial(settle_kernel, sizes, [[skip for x, skip in held] for held, size in runs]),
        [(sum(sizes), DK, W2)],
        "settle",
        [x for held, size in runs for x, skip in held],
        after,
    )
    return out


def slot_rows_kernel(slots, n_prompt, sb_ref, bl_ref, bp_ref, *refs):
    out_ref = refs[-1]
    me = lax.axis_index("prompt")
    rank = lax.axis_index("seq") * n_prompt + me
    for slot in range(slots):
        branch = sb_ref[rank * slots + slot]
        mine = jnp.where(bp_ref[branch] == me, 1, 0)
        out_ref[slot, 0:8] = jnp.full((8, W2), bl_ref[branch], jnp.int32)
        out_ref[slot, 8:16] = jnp.full((8, W2), mine, jnp.int32)


def slot_rows(slots, tables, after):
    return pl.pallas_call(
        functools.partial(slot_rows_kernel, slots, lax.axis_size("prompt")),
        in_specs=[pl.BlockSpec(memory_space=pltpu.SMEM)] * 3 + [ANY] * len(after),
        out_specs=WHOLE,
        out_shape=pltpu.VMEM((slots, 16, W2), jnp.int32),
        compiler_params=pltpu.CompilerParams(vmem_limit_bytes=SCOPED),
        cost_estimate=SHORT,
        name="slot_rows",
    )(*tables, *after)


def finish(a, state, b, gain2):
    raw = mm(a, diag2(low16(state))) + b.astype(jnp.float32)
    share = diag2(jnp.full((DV, W2), 1.0 / DV, jnp.bfloat16))
    return raw * lax.rsqrt(mm(low16(raw * raw), share) + EPS_NORM) * gain2


def suffix_out_kernel(sizes, *refs):
    rows_ref, own_ref, other_ref, gain_ref = refs[:4]
    out_ref = refs[-1]
    slot = pl.program_id(0)
    mine = rows_ref[slot, 8:9] == 1
    gain = gain_ref[...]
    gain2 = jnp.concatenate([gain, gain], axis=1)
    tokens = out_ref.shape[1]
    live = lax.broadcasted_iota(jnp.int32, (tokens, W2), 0) < rows_ref[slot, 0:1]
    for p, (run, at) in enumerate(places_of(sizes)):
        source = slice(at * W2, (at + 1) * W2)
        a_ref, b_ref = refs[4 + 2 * run : 6 + 2 * run]
        state = jnp.where(mine, own_ref[p], other_ref[p])
        out = finish(a_ref[slot, :, source], state, b_ref[slot, :, source], gain2)
        out_ref[0, :, p * W2 : (p + 1) * W2] = low16(jnp.where(live, out, 0.0))


def suffix_outputs(first, rows, own, other, terms, gain, so_far, width, after=()):
    slots, tokens, _ = terms[0][0].shape
    sizes = [a.shape[2] // W2 for a, b in terms]
    pairs = sum(sizes)
    at = first // pairs
    args = [rows, own, other, gain] + [x for pair in terms for x in pair]
    in_specs = [WHOLE] * len(args)
    args = [near(value) for value in args]
    aliases = {}
    if so_far is not None:
        aliases = {len(args): 0}
        in_specs.append(ANY)
        args.append(away(so_far))
    return pl.pallas_call(
        functools.partial(suffix_out_kernel, sizes),
        grid=(slots,),
        in_specs=in_specs + [ANY] * len(after),
        out_specs=pl.BlockSpec((1, tokens, pairs * W2), lambda i: (i, 0, at)),
        out_shape=pltpu.HBM((slots, tokens, width), jnp.bfloat16),
        input_output_aliases=aliases,
        compiler_params=pltpu.CompilerParams(vmem_limit_bytes=SCOPED),
        cost_estimate=SHORT,
        name="suffix_out",
    )(*args, *after)


def prompt_out_kernel(calls, hops, *refs):
    here = lax.axis_index("seq")
    refs, out_ref, state_ref = list(refs[:-2]), refs[-2], refs[-1]
    for j, sizes in enumerate(hops):
        arrived = [refs.pop(0) for _ in sizes]

        @pl.when((here == j + 1) | ((here == 0) & (j == 0)))
        def _(sizes=sizes, arrived=arrived):
            for p, (run, at) in enumerate(places_of(sizes)):
                state_ref[p] = pair_at(arrived[run], at)

    terms = [(refs.pop(0), refs.pop(0)) for _ in calls]
    gain = refs[0][...]
    gain2 = jnp.concatenate([gain, gain], axis=1)
    for p, (call, at) in enumerate(places_of(calls)):
        source = slice(at * W2, (at + 1) * W2)
        a_ref, b_ref = terms[call]
        out = finish(a_ref[:, source], state_ref[p], b_ref[:, source], gain2)
        out_ref[0, :, p * W2 : (p + 1) * W2] = low16(out)


def first_out_kernel(calls, hops, count, sizes, *refs):
    prompt_ref, suffix_ref, state_ref = refs[-3:]

    @pl.when(pl.program_id(0) == 0)
    def _():
        prompt_out_kernel(calls, hops, *refs[:count], prompt_ref, state_ref)

    stop = count + 4 + 2 * len(sizes)
    suffix_out_kernel(sizes, *refs[count:stop], suffix_ref)


def first_outputs(arrived, terms, rows, own, other, made, gain, width, after):
    pairs = width // W2
    slots, tokens, _ = made[0][0].shape
    calls = [a.shape[1] // W2 for a, b in terms]
    hops = [[size for x, size in hop] for hop in arrived]
    sizes = [a.shape[2] // W2 for a, b in made]
    args = [x for hop in arrived for x, size in hop] + [x for pair in terms for x in pair] + [gain]
    count = len(args)
    args += [rows, own, other, gain] + [x for pair in made for x in pair]
    return pl.pallas_call(
        functools.partial(first_out_kernel, calls, hops, count, sizes),
        grid=(slots,),
        in_specs=[WHOLE] * len(args) + [ANY] * len(after),
        out_specs=[
            pl.BlockSpec((1, CH, width), lambda i: (0, 0, 0)),
            pl.BlockSpec((1, tokens, sum(sizes) * W2), lambda i: (i, 0, 0)),
        ],
        out_shape=[
            pltpu.HBM((1, CH, width), jnp.bfloat16),
            pltpu.HBM((slots, tokens, width), jnp.bfloat16),
        ],
        scratch_shapes=[pltpu.VMEM((pairs, DK, W2), jnp.float32)],
        compiler_params=pltpu.CompilerParams(vmem_limit_bytes=SCOPED),
        cost_estimate=SHORT,
        name="first_out",
    )(*[near(value) for value in args], *after)


def pair_product(left, right):
    pairs = left.shape[0]
    left = left.reshape(pairs, DK, 2, DK)
    right = right.reshape(pairs, DK, 2, DV)
    return jnp.einsum("pihj,pjhv->pihv", left, right, precision=HIGH).reshape(pairs, DK, W2)


def send(value, source, target):
    return lax.ppermute(value, "seq", [(source, target)])


class Forward:
    def __init__(self, boths, arrived, skip):
        self.boths, self.size = boths, sum(both.shape[1] for both in boths)
        self.skip = skip
        self.arrived, self.states = [arrived], []

    def advance(self, after):
        hop = len(self.states)
        state = step(hop + 1, self.boths, self.arrived[-1], after, 0 if hop else self.skip)
        self.states.append(state)
        count = lax.axis_size("seq")
        if hop + 2 < count and not (count == 4 and hop == 1):
            self.arrived.append(send(state, hop + 1, hop + 2))
        return (near(state),)


class Backward:
    def __init__(self, both, arrived, direct):
        self.both, self.size, self.direct, self.right = both, both.shape[1], direct, None
        count = lax.axis_size("seq")
        self.half = count // 2
        here = lax.axis_index("seq")
        self.far = arrived
        for source in range(count - 2, self.half, -1):
            sending = jnp.stack(
                [
                    pair_product(arrived[0], both[0]),
                    pair_product(arrived[0], both[1]) + arrived[1],
                ]
            )
            arrived = send(sending, source, source - 1)
            self.far = jnp.where(here == source - 1, arrived, self.far)

    def meet(self, after):
        half = self.half
        state = self.run.states[half - 1]
        self.mid = meet(half, self.far, self.skip, state, after)
        self.lefts = [send(self.mid, half, half - 1)]
        if self.direct:
            self.lefts = [send(self.mid, half, d) for d in range(half - 1)] + self.lefts
        elif half > 2:
            for d in range(half - 2, -1, -1):
                self.lefts.insert(0, send(self.lefts[0], d + 1, d))
        return (near(self.mid),)

    def pass_on(self, after):
        right = (self.run.states[self.half - 1], self.skip)
        left = right if self.direct else (self.lefts[0], 0)
        out = part(self.half, self.size, left, right, after)
        if self.direct:
            self.right = send(out, self.half, self.half + 1)
        else:
            self.right = lax.ppermute(out, "seq", [(1, 0), (2, 3)])
            self.lefts.insert(0, self.right)
        return (near(out),)

    def reach_end(self, after):
        if self.half == 2:
            self.end = step(3, [self.both], self.right, after)
            return (near(self.end),)
        while len(self.run.states) < lax.axis_size("seq") - 1:
            after = self.run.advance(after)
        return after

    def held(self):
        if self.half == 2:
            ends = [(self.end, 0)]
        else:
            ends = [(state, self.skip) for state in self.run.states[self.half :]]
        return [(left, 0) for left in self.lefts] + [(self.mid, 0)] + ends


def settle_runs(backs, after):
    half, count, here = backs[0].half, lax.axis_size("seq"), lax.axis_index("seq")
    final = settle([(back.held(), back.size) for back in backs], after)
    if half > 2:
        inner = (here > half) & (here < count - 1)
        far = jnp.concatenate([back.far for back in backs], axis=1)
        final = jnp.where(inner, pair_product(far[0], final) + far[1], final)
    prompts = lax.axis_size("prompt")
    other = lax.ppermute(final, "prompt", [(i, (i + 1) % prompts) for i in range(prompts)])
    return final, other


def plan_of(pairs):
    if pairs % 8:
        return [[1]] * pairs, [[1]] * pairs, [1] * pairs, [(pairs, pairs)], 0
    u = pairs // 4
    return [[u, u], [u, u // 2, u // 2]], [[2], [2], [1]], [u] * 4, [(2, 2), (3, 2)], 1


FIVE = (
    ("forward", 0),
    ("make", 0),
    ("make", 0),
    ("forward", 1),
    ("forward", 0),
    ("meet", 0),
    ("meet", 1),
    ("pass", 0),
    ("forward", 2),
    ("forward", 1),
    ("meet", 2),
    ("pass", 1),
    ("meet", 3),
    ("end", 0),
    ("forward", 2),
    ("pass", 4),
    ("meet", 4),
    ("pass", 2),
    ("pass", 3),
    ("make", 0),
    ("end", 1),
    ("settle", 0),
    ("land", 4),
    ("end", 2),
    ("end", 3),
    ("end", 4),
    ("settle", 1),
    ("prompt", 0),
    ("out", 1),
)


def order_of(joins, half, makes, groups):
    if half == 2 and joins == [[2], [2], [1]]:
        return FIVE
    forwards, runs = sum(len(join) for join in joins), sum(sum(join) for join in joins)
    order = [("forward", k) for j in range(half) for k in range(forwards)]
    order += [("meet", k) for k in range(runs)]
    order += [("pass", k) for k in range(runs) if half == 2]
    order += [("make", k) for k in range(makes)]
    order += [("end", k) for k in range(runs)]
    order += [("settle", k) for k in range(groups)] + [("prompt", 0)]
    return order + [("out", k) for k in range(1, groups)]


def local(
    prompt_queries,
    prompt_keys,
    prompt_values,
    prompt_beta,
    prompt_decay,
    suffix_queries,
    suffix_keys,
    suffix_values,
    suffix_beta,
    suffix_decay,
    norm_gain,
    slot_branch,
    branch_length,
    branch_prompt,
):
    gain = norm_gain.reshape(1, DV)
    tables = (slot_branch, branch_length, branch_prompt)
    width = prompt_values.shape[2]
    prompt_in = (prompt_queries, prompt_keys, prompt_values, prompt_beta, prompt_decay)
    suffix_in = (suffix_queries, suffix_keys, suffix_values, suffix_beta, suffix_decay)
    half = lax.axis_size("seq") // 2

    calls, joins, units, groups, direct = plan_of(width // W2)
    total = sum(len(sizes) for sizes in calls)
    boths, terms, packed = [], [], []
    heads_of = [(k, size) for k, join in enumerate(joins) for size in join]
    bounds = [sum(size for k, size in heads_of[:i]) for i in range(len(heads_of) + 1)]

    def pack_up(after):
        while len(packed) < len(boths):
            k = len(packed)
            start = sum(sum(join) for join in joins[:k])
            stop = sum(sum(join) for join in joins[: k + 1])
            if len(boths) < stop:
                break
            packed.append(pack(half, boths[start:stop], boths[k], after))
            after = (near(packed[-1]),)
        return after

    made = []

    def make(after):
        if len(made) == len(units):
            return after
        unit = units[len(made)]
        made.append(suffix_terms(sum(units[: len(made)]), unit, *suffix_in, after=after))
        return (near(made[-1][0]),)

    first, last = 0, ()
    for call, sizes in enumerate(calls):
        new, a, b = prompt_terms(first, sizes, *prompt_in, after=last)
        boths += new
        terms.append((a, b))
        last = pack_up((near(a),))
        if call == 0:
            last = make(last)
        first += sum(sizes)
    opened = [
        lax.ppermute(out, "seq", [(0, 1), (2 * half - 1, 2 * half - 2)]) for out in packed
    ]
    forwards = []
    for i, (k, size) in enumerate(heads_of):
        start = sum(sum(join) for join in joins[:k])
        skip = sum(x.shape[1] for x in boths[start : bounds[i]])
        forwards.append(Forward(boths[bounds[i] : bounds[i + 1]], opened[k], skip))
    backwards = []
    for k, both in enumerate(boths):
        back = Backward(both, opened[k], k + direct >= total)
        f = [i for i in range(len(heads_of)) if bounds[i] <= k][-1]
        back.run = forwards[f]
        back.skip = sum(x.shape[1] for x in boths[bounds[f] : k])
        back.first = sum(x.shape[1] for x in boths[:k])
        backwards.append(back)
    rows = slot_rows(suffix_queries.shape[0], tables, last)
    last = (near(rows),)
    settled = {}
    edges = [sum(runs for runs, count in groups[:i]) for i in range(len(groups) + 1)]
    prompt_out, suffix_out = None, None
    for what, k in order_of(joins, half, len(units), len(groups)):
        if what == "make":
            last = make(last)
        elif what == "forward":
            last = forwards[k].advance(last)
        elif what == "meet":
            last = backwards[k].meet(last)
        elif what == "pass":
            last = backwards[k].pass_on(last)
        elif what == "land":
            last = last + tuple(near(left) for left in backwards[k].lefts)
        elif what == "end":
            last = backwards[k].reach_end(last)
        elif what == "settle":
            settled[k] = settle_runs(backwards[edges[k] : edges[k + 1]], last)
            last = (near(settled[k][0]),)
        elif what == "out":
            done = sum(count for runs, count in groups[:k])
            suffix_out = suffix_outputs(
                backwards[edges[k]].first,
                rows,
                *settled[k],
                made[done : done + groups[k][1]],
                gain,
                suffix_out,
                width,
                last if k == 0 else (),
            )
            last = (away(suffix_out),)
        else:
            lots = [sum(f.size for f, (i, n) in zip(forwards, heads_of) if i == k) for k in range(len(joins))]
            came = [list(zip(opened, lots))]
            for j in range(1, len(forwards[0].arrived)):
                came.append([(f.arrived[j], f.size) for f in forwards])
            if half == 2:
                came.append([(back.right, back.size) for back in backwards])
            done = groups[0][1]
            prompt_out, suffix_out = first_outputs(
                came, terms, rows, *settled[0], made[:done], gain, width, last
            )
            last = (away(prompt_out),)
    return (prompt_out, suffix_out)


def solution(mesh):
    return jax.shard_map(
        local,
        mesh=mesh,
        in_specs=(
            P(("groups", "prompt"), "seq", "head"),
            P(("groups", "prompt"), "seq", "head"),
            P(("groups", "prompt"), "seq", "head"),
            P(("groups", "prompt"), "head", "seq"),
            P(("groups", "prompt"), "head", "seq"),
            P(("groups", "seq", "prompt"), None, "head"),
            P(("groups", "seq", "prompt"), None, "head"),
            P(("groups", "seq", "prompt"), None, "head"),
            P(("groups", "seq", "prompt"), "head", None),
            P(("groups", "seq", "prompt"), "head", None),
            P(),
            P("groups"),
            P("groups"),
            P("groups"),
        ),
        out_specs=(
            P(("groups", "prompt"), "seq", "head"),
            P(("groups", "seq", "prompt"), None, "head"),
        ),
        check_vma=False,
    )
```
